512 devices in a mesh: dp: 8 (over x, z_lo), seq: 8 (over z_hi, core), head: 8 (over y).
Axes of the slice: x: 4, y: 8, z: 8 (z_hi: 4, z_lo: 2; z = z_hi * 2 + z_lo), core: 2. Of those that a mesh axis runs over, the one named last changes fastest.
Arguments:
- patch_in: bfloat16 [8, 1024, 1536], P('dp', 'head', 'seq'), may hold values from -6 to 6
- enc_weight: bfloat16 [1536, 1536], P('seq'), may hold values from -0.15625 to 0.15625
- enc_gain: float32 [1536], replicated, may hold values from 0.1 to 1.9
- enc_bias: float32 [1536], replicated, may hold values from -3 to 3
- interp_index: int32 [8, 2304], P('dp', 'seq'), may hold values from 0 to 1023, as said below
- queries: bfloat16 [8, 2304, 3072], P('dp', 'seq', 'head'), may hold values from -64 to 64
- key_rows: bfloat16 [8, 2304, 3072], P('dp', 'seq', 'head'), may hold values from -64 to 64
- value_rows: bfloat16 [8, 2304, 3072], P('dp', 'seq', 'head'), may hold values from -6 to 6
- proj_weight: bfloat16 [1536, 3072], P(None, 'head'), may hold values from -0.109375 to 0.109375
Outputs:
- attn_out: bfloat16 [8, 2304, 3072], P('dp', 'seq', 'head')
- cosine: float32 [8, 2304], P('dp', 'seq')
- grad_attn: bfloat16 [8, 2304, 3072], P('dp', 'seq', 'head')
- grad_proj: float32 [1536, 3072], P(('dp', 'seq'), 'head')
The draws below stay inside these ranges and needn't reach their ends.
Inputs may be any that keep to these rules, and one draw needn't show every extreme that they name: interp_index[b, t] names a patch of the same sample's crop.
All inputs are finite; a program needn't handle non-finite values.
Results may differ from the reference program's by a relative error of at most 0.017.
Values may be sent and summed in bfloat16 or wider, within the bound.
A program may use at most 64 MiB of HBM per device.

```python
import jax
import jax.numpy as jnp
from jax import lax

E = 1536
HEADS = 24
HD = 128
PSIDE = 32
LAT_SIDE = 48
SAMPLES = 8
TOKENS = 2304
PATCH = 1024
DA = 3072
N_SEQ = 8


def draw_interp_index(key, part):
    key = jax.random.fold_in(key, 3)
    offsets = jax.random.randint(key, (SAMPLES, 2), 0, PSIDE, dtype=jnp.int32)
    positions = jnp.arange(TOKENS, dtype=jnp.int32)
    lat_row = positions // LAT_SIDE * PSIDE // LAT_SIDE
    lat_col = positions % LAT_SIDE * PSIDE // LAT_SIDE
    patch_row = (lat_row[None, :] + offsets[:, 0:1]) % PSIDE
    patch_col = (lat_col[None, :] + offsets[:, 1:2]) % PSIDE
    return (patch_row * PSIDE + patch_col).astype(jnp.int32)


def draw_key_rows(key, part):
    key = jax.random.fold_in(key, 5)
    drawn = jax.random.normal(key, (SAMPLES, TOKENS, DA), jnp.float32) * 1.5
    return drawn.astype(jnp.bfloat16)


def draw_queries(key, part):
    key = jax.random.fold_in(key, 7)
    drawn = jax.random.normal(key, (SAMPLES, TOKENS, DA), jnp.float32) * 1.5
    return drawn.astype(jnp.bfloat16)


def shard_levels(rng, dims, cuts, least, high):
    loudness, own = 1.0, jax.random.fold_in(rng, 6)
    for axis_at, parts in cuts:
        draws = jnp.exp(jax.random.uniform(jax.random.fold_in(own, axis_at), (parts,), jnp.float32, least / len(cuts), high / len(cuts)))
        loudness = loudness * jnp.repeat(draws, dims[axis_at] // parts).reshape([-1 if axis == axis_at else 1 for axis in range(len(dims))])
    return loudness


def scatter_about(rng, extent, scale, reach, shards=(), kind=jnp.bfloat16):
    drawn = scale * jax.random.normal(rng, extent, jnp.float32)
    if shards:
        drawn = drawn * shard_levels(rng, extent, shards, -0.22, 0.18)
    return jnp.clip(drawn, -reach, reach).astype(kind)


def setup_inputs(seed: int = 0) -> dict:
    keys = jax.random.split(jax.random.key(seed), 10)
    patch_in = scatter_about(keys[0], (SAMPLES, PATCH, E), 1.0, 6.0, ((0, 8), (1, 8), (2, 8)))
    enc_weight = scatter_about(keys[1], (E, E), E ** -0.5, 0.15625, ((0, 8),))
    enc_gain = jnp.clip(1.0 + 0.18 * jax.random.normal(keys[2], (E,), jnp.float32), 0.1, 1.9)
    enc_bias = scatter_about(keys[3], (E,), 0.5, 3.0, (), jnp.float32)
    interp_index = draw_interp_index(jax.random.fold_in(keys[9], 71), 0)
    queries = draw_queries(jax.random.fold_in(keys[9], 71), 0)
    key_rows = draw_key_rows(jax.random.fold_in(keys[9], 71), 0)
    value_rows = scatter_about(keys[7], (SAMPLES, TOKENS, DA), 1.0, 6.0, ((0, 8), (1, 8), (2, 8)))
    proj_weight = scatter_about(keys[8], (E, DA), DA ** -0.5, 0.109375, ((1, 8),))
    return dict(patch_in=patch_in, enc_weight=enc_weight, enc_gain=enc_gain, enc_bias=enc_bias, interp_index=interp_index, queries=queries, key_rows=key_rows, value_rows=value_rows, proj_weight=proj_weight)


layer_eps = 1e-06
cos_eps = 1e-06

def normalize(encoded, enc_gain, enc_bias):
    average = lax.optimization_barrier(jnp.mean(encoded, axis=-1, keepdims=True))
    centred = encoded - average
    variance = lax.optimization_barrier(jnp.mean(centred * centred, axis=-1, keepdims=True))
    return (centred * lax.rsqrt(variance + layer_eps) * enc_gain + enc_bias).astype(jnp.bfloat16)

def reference(patch_in, enc_weight, enc_gain, enc_bias, interp_index, queries, key_rows, value_rows, proj_weight):

    def encode_one(patches):
        encoded = jnp.dot(patches, enc_weight, preferred_element_type=jnp.float32)
        return normalize(encoded, enc_gain, enc_bias)
    targets = lax.map(encode_one, patch_in)
    aligned = jax.vmap(lambda table, picks: table[picks])(targets, interp_index)
    aligned = aligned.reshape(SAMPLES * TOKENS, E).astype(jnp.float32)
    score_scale = HD ** (-0.5)
    block_rows = TOKENS // N_SEQ

    def split_heads(array):
        return array.reshape(SAMPLES, TOKENS, HEADS, HD).transpose(0, 2, 1, 3).reshape(SAMPLES * HEADS, TOKENS, HD)

    def attend_head(operands):
        q_head, k_head, v_head = operands
        q_blocks = q_head.reshape(TOKENS // block_rows, block_rows, HD)

        def attend_block(q_block):
            scores = jnp.dot(q_block, k_head.T, preferred_element_type=jnp.float32) * score_scale
            row_max = lax.optimization_barrier(jnp.max(scores, axis=1, keepdims=True))
            exponent = jnp.exp(scores - row_max)
            probs = (exponent / lax.optimization_barrier(jnp.sum(exponent, axis=1, keepdims=True))).astype(jnp.bfloat16)
            return jnp.dot(probs, v_head, preferred_element_type=jnp.float32).astype(jnp.bfloat16)
        return lax.map(attend_block, q_blocks).reshape(TOKENS, HD)
    head_outs = lax.map(attend_head, (split_heads(queries), split_heads(key_rows), split_heads(value_rows)))
    attn_out = head_outs.reshape(SAMPLES, HEADS, TOKENS, HD).transpose(0, 2, 1, 3).reshape(SAMPLES, TOKENS, DA)
    flat_attn = attn_out.reshape(SAMPLES * TOKENS, DA)
    projected = jnp.dot(flat_attn, proj_weight.T, preferred_element_type=jnp.float32)
    proj_norm = jnp.sqrt(lax.optimization_barrier(jnp.sum(projected * projected, axis=1)) + cos_eps)
    aligned_norm = jnp.sqrt(lax.optimization_barrier(jnp.sum(aligned * aligned, axis=1)) + cos_eps)
    cosine = lax.optimization_barrier(jnp.sum(projected * aligned, axis=1)) / (proj_norm * aligned_norm)
    grad_projected = (-(aligned / (proj_norm * aligned_norm)[:, None] - (cosine / (proj_norm * proj_norm))[:, None] * projected)).astype(jnp.bfloat16)
    grad_attn = jnp.dot(grad_projected, proj_weight, preferred_element_type=jnp.float32).astype(jnp.bfloat16)
    grad_proj = jnp.dot(grad_projected.T, flat_attn, preferred_element_type=jnp.float32)
    return (attn_out, cosine.reshape(SAMPLES, TOKENS), grad_attn.reshape(SAMPLES, TOKENS, DA), grad_proj)
```

```python
import jax
import jax.numpy as jnp
from jax import lax
from jax.experimental import pallas as pl
from jax.experimental.pallas import tpu as pltpu
from jax.sharding import PartitionSpec as P

MESH = pl.DeviceIdType.MESH
BF = jnp.bfloat16
F32 = jnp.float32

E = 1536
HD = 128
NH = 3
DA = NH * HD
TOK = 288
HALF = 144
SUB = 48
PHASES = 3
EC = 384

layer_eps = 1e-06
cos_eps = 1e-06


def remote(src, dst, send, recv, where):
    return pltpu.make_async_remote_copy(
        src_ref=src, dst_ref=dst, send_sem=send, recv_sem=recv, device_id=where, device_id_type=MESH
    )


def greet(peers):
    barrier = pltpu.get_barrier_semaphore()
    for peer in peers:
        pl.semaphore_signal(barrier, inc=1, device_id=peer, device_id_type=MESH)
    pl.semaphore_wait(barrier, len(peers))


def places():
    dp, seq, y = lax.axis_index("dp"), lax.axis_index("seq"), lax.axis_index("head")
    return dp // 2, dp % 2, seq // 2, seq % 2, y


def front(
    patch, enc_w, gain, bias, idx, q, k, v, attn, aligned,
    kbuf, vbuf, part, e1r, e2s, e2r, e3s, e3r, tgt, table,
    k_s, k_r, v_s, v_r, e_s, e_r, t_s, t_r, g_s, g_r,
):
    x, zl, zh, c, y = places()
    seq = zh * 2 + c
    up, dn, op = (zh + 1) % 4, (zh + 3) % 4, (zh + 2) % 4
    at_up, at_dn, at_sib = {"seq": up * 2 + c}, {"seq": dn * 2 + c}, {"seq": zh * 2 + 1 - c}
    s_up, s_dn, s_op = up * 2 + c, dn * 2 + c, op * 2 + c
    o = 1 - c
    sent = []

    def go(copy):
        copy.start()
        sent.append(copy)

    greet([at_up, at_dn, at_sib] + [{"head": (y + d) % 8} for d in range(1, 8)])

    def own(h):
        cols = slice(h * HD, (h + 1) * HD)
        for n, (src, buf, ss, rs) in enumerate(((k, kbuf, k_s, k_r), (v, vbuf, v_s, v_r))):
            for w, where in enumerate((at_up, at_dn, at_sib)):
                go(remote(src.at[:, cols], buf.at[h, seq], ss.at[h, w], rs.at[h, seq], where))
            buf[h, seq] = src[:, cols]

    def landed(buf, rs, h, s):
        remote(buf.at[h, s], buf.at[h, s], rs.at[h, s], rs.at[h, s], at_sib).wait_recv()

    def forward(buf, ss, rs, h, s, w, where):
        go(remote(buf.at[h, s], buf.at[h, s], ss.at[h, w], rs.at[h, s], where))

    def relay(h):
        landed(kbuf, k_r, h, s_dn)
        forward(kbuf, k_s, k_r, h, s_dn, 3, at_up)
        forward(kbuf, k_s, k_r, h, s_dn, 4, at_sib)
        landed(vbuf, v_r, h, s_up)
        forward(vbuf, v_s, v_r, h, s_up, 3, at_dn)
        forward(vbuf, v_s, v_r, h, s_up, 4, at_sib)
        landed(vbuf, v_r, h, s_dn)
        forward(vbuf, v_s, v_r, h, s_dn, 5, at_sib)
        landed(kbuf, k_r, h, s_up)
        forward(kbuf, k_s, k_r, h, s_up, 5, at_sib)

    def finish(h):
        landed(kbuf, k_r, h, s_op)
        forward(kbuf, k_s, k_r, h, s_op, 6, at_sib)
        landed(vbuf, v_r, h, s_op)
        forward(vbuf, v_s, v_r, h, s_op, 6, at_sib)

    def attend(h):
        for z in range(4):
            landed(kbuf, k_r, h, z * 2 + o)
        for z in range(4):
            landed(vbuf, v_r, h, z * 2 + o)
        keys = kbuf.at[h]
        values = vbuf.at[h]

        @pl.loop(0, 3)
        def _(b):
            rows = pl.ds(pl.multiple_of(b * 96, 96), 96)
            kk = keys[...].reshape(8 * TOK, HD)
            vv = values[...].reshape(8 * TOK, HD)
            scores = lax.dot_general(
                q[rows, h * HD : (h + 1) * HD], kk, (((1,), (1,)), ((), ())),
                preferred_element_type=F32,
            )
            top = jnp.max(scores, axis=1, keepdims=True)
            expo = jnp.exp((scores - top) * (HD**-0.5))
            total = jnp.sum(expo, axis=1, keepdims=True)
            out = jnp.dot(expo.astype(BF), vv, preferred_element_type=F32)
            attn[rows, h * HD : (h + 1) * HD] = (out / total).astype(BF)

    own(0)
    share = jnp.dot(patch[...], enc_w[...], preferred_element_type=F32)
    for z in range(4):
        for cc in range(2):
            part[z, cc] = share[(2 * z + cc) * 16 : (2 * z + cc + 1) * 16]
    for z in range(4):
        go(remote(part.at[z, o], e1r.at[z], e_s.at[z], e_r.at[z], at_sib))
    for z in range(4):
        remote(part.at[z, o], e1r.at[z], e_s.at[z], e_r.at[z], at_sib).wait_recv()
    far = part[op, c] + e1r[op]
    e2s[0] = far[:, : E // 2].astype(BF)
    e2s[1] = far[:, E // 2 :].astype(BF)
    go(remote(e2s.at[0], e2r.at[0], e_s.at[4], e_r.at[4], at_up))
    go(remote(e2s.at[1], e2r.at[1], e_s.at[5], e_r.at[5], at_dn))
    own(1)
    remote(e2s.at[0], e2r.at[0], e_s.at[4], e_r.at[4], at_up).wait_recv()
    remote(e2s.at[1], e2r.at[1], e_s.at[5], e_r.at[5], at_dn).wait_recv()
    near = part[up, c] + e1r[up]
    e3s[0, :, : E // 2] = (near[:, : E // 2] + e2r[0].astype(F32)).astype(BF)
    e3s[0, :, E // 2 :] = near[:, E // 2 :].astype(BF)
    near = part[dn, c] + e1r[dn]
    e3s[1, :, : E // 2] = near[:, : E // 2].astype(BF)
    e3s[1, :, E // 2 :] = (near[:, E // 2 :] + e2r[1].astype(F32)).astype(BF)
    go(remote(e3s.at[0], e3r.at[0], e_s.at[6], e_r.at[6], at_up))
    go(remote(e3s.at[1], e3r.at[1], e_s.at[7], e_r.at[7], at_dn))
    relay(0)
    own(2)
    remote(e3s.at[0], e3r.at[0], e_s.at[6], e_r.at[6], at_up).wait_recv()
    remote(e3s.at[1], e3r.at[1], e_s.at[7], e_r.at[7], at_dn).wait_recv()
    enc = part[zh, c] + e1r[zh] + e3r[0].astype(F32) + e3r[1].astype(F32)
    average = jnp.mean(enc, axis=1, keepdims=True)
    centred = enc - average
    variance = jnp.mean(centred * centred, axis=1, keepdims=True)
    normed = (
        centred * lax.rsqrt(variance + layer_eps) * gain[...].reshape(1, E) + bias[...].reshape(1, E)
    ).astype(BF)
    for n in range(4):
        tgt[n] = normed[:, n * EC : (n + 1) * EC]
    for d in range(1, 8):
        to = (y + d) % 8
        go(remote(tgt.at[to % 4], table.at[seq, y], t_s.at[d], t_r.at[8 - d], {"head": to}))
    table[seq, y] = tgt[y % 4]
    relay(1)
    for d in range(1, 8):
        fr = (y + d) % 8
        remote(tgt.at[0], table.at[seq, fr], t_s.at[d], t_r.at[d], {"head": fr}).wait_recv()
    for w, where in enumerate((at_up, at_dn, at_sib)):
        go(remote(table.at[seq], table.at[seq], g_s.at[w], g_r.at[seq], where))
    finish(0)
    attend(0)
    relay(2)

    def took(s):
        remote(table.at[s], table.at[s], g_r.at[s], g_r.at[s], at_sib).wait_recv()

    took(s_dn)
    go(remote(table.at[s_dn, :4], table.at[s_dn, :4], g_s.at[3], g_r.at[s_dn], at_up))
    go(remote(table.at[s_dn], table.at[s_dn], g_s.at[4], g_r.at[s_dn], at_sib))
    took(s_up)
    go(remote(table.at[s_up, 4:], table.at[s_up, 4:], g_s.at[5], g_r.at[8], at_dn))
    go(remote(table.at[s_up], table.at[s_up], g_s.at[6], g_r.at[s_up], at_sib))
    finish(1)
    attend(1)
    finish(2)
    remote(table.at[s_op, :4], table.at[s_op, :4], g_s.at[3], g_r.at[s_op], at_up).wait_recv()
    remote(table.at[s_op, 4:], table.at[s_op, 4:], g_s.at[5], g_r.at[8], at_dn).wait_recv()
    go(remote(table.at[s_op], table.at[s_op], g_s.at[7], g_r.at[s_op], at_sib))
    attend(2)
    for z in range(4):
        took(z * 2 + o)
    picks = idx[...]
    spot = (picks % 128) // 16 * 128 + picks // 128 * 16 + picks % 16
    hot = (lax.broadcasted_iota(jnp.int32, (1024, TOK), 0) == spot).astype(F32).astype(BF)
    aligned[...] = lax.dot_general(
        hot, table[...].reshape(1024, EC), (((0,), (0,)), ((), ())), preferred_element_type=F32
    )
    for copy in sent:
        copy.wait_send()


def tail(
    attn, w, aligned, cos_out, grad_attn, grad_proj,
    part, a_sb, a_rb, b_sb, b_rb, stat, cosx, gp, r1s, r1r, own, r2s, r2r, r2h, r3s, r3r, r4s,
    ss_a, rs_a, ss_b, rs_b, ss_st, rs_st, ss_c, rs_c, ss_g, rs_g, ss_r, rs_r, ss_z, rs_z,
):
    x, zl, zh, c, y = places()
    th, ec = y // 4, y % 4
    odd = y % 2
    nxt, prv = (y + 1) % 8, (y + 7) % 8
    buddy = y + 2 * odd - 1
    buddy = (buddy + 8) % 8
    o = 1 - c
    at_sib = {"seq": zh * 2 + o}
    xu, xd, xo = (x + 1) % 4, (x + 3) % 4, (x + 2) % 4
    at_xu, at_xd = {"dp": xu * 2 + zl}, {"dp": xd * 2 + zl}
    sent = []

    def go(copy):
        copy.start()
        sent.append(copy)

    zpeers = []
    for d in range(1, 8):
        zz = (zh * 2 + zl + d) % 8
        zpeers.append({"dp": x * 2 + zz % 2, "seq": zz // 2 * 2 + c})
    greet([at_sib, at_xu, at_xd] + [{"head": (y + d) % 8} for d in range(1, 8)] + zpeers)

    partial = lax.dot_general(
        attn[...], w[...], (((1,), (1,)), ((), ())), preferred_element_type=F32
    )
    for i in range(PHASES):
        for t in range(2):
            for e in range(4):
                part[i, t * 4 + e] = partial[
                    t * HALF + i * SUB : t * HALF + (i + 1) * SUB, e * EC : (e + 1) * EC
                ]
    for i in range(PHASES):
        a_sb[i] = part[i, (y + 4) % 8].astype(BF)
        go(remote(a_sb.at[i], a_rb.at[i], ss_a.at[i], rs_a.at[i], {"head": buddy_of(y, odd)}))
    for i in range(PHASES):
        remote(a_sb.at[i], a_rb.at[i], ss_a.at[i], rs_a.at[i], {"head": nxt}).wait_recv()
        got = a_rb[i].astype(F32)
        far_p = part[i, (y + 3) % 8]
        far_m = part[i, (y + 5) % 8]
        b_sb[i, 0, 0] = jnp.where(odd == 1, far_p + got, far_p).astype(BF)
        b_sb[i, 0, 1] = jnp.where(odd == 1, far_m, far_m + got).astype(BF)
        go(remote(b_sb.at[i, 0, 0], b_rb.at[i, 0, 0], ss_b.at[i, 0, 0], rs_b.at[i, 0, 0], {"head": nxt}))
        go(remote(b_sb.at[i, 0, 1], b_rb.at[i, 0, 1], ss_b.at[i, 0, 1], rs_b.at[i, 0, 1], {"head": prv}))
    for s in range(1, 3):
        for i in range(PHASES):
            for side, where in ((0, nxt), (1, prv)):
                remote(b_sb.at[i, s - 1, side], b_rb.at[i, s - 1, side], ss_b.at[i, s - 1, side],
                       rs_b.at[i, s - 1, side], {"head": where}).wait_recv()
                to = (y + 3 - s) % 8 if side == 0 else (y + 5 + s) % 8
                b_sb[i, s, side] = (part[i, to] + b_rb[i, s - 1, side].astype(F32)).astype(BF)
                go(remote(b_sb.at[i, s, side], b_rb.at[i, s, side], ss_b.at[i, s, side],
                          rs_b.at[i, s, side], {"head": where}))

    def rows_of(i):
        return pl.ds(pl.multiple_of(th * HALF + i * SUB, 16), SUB)

    lane = lax.broadcasted_iota(jnp.int32, (128, 128), 1)
    sub = lax.broadcasted_iota(jnp.int32, (128, 128), 0)

    def fill(column):
        return jnp.concatenate([column, jnp.zeros((128 - SUB, 1), F32)], axis=0)

    for i in range(PHASES):
        for side, where in ((0, nxt), (1, prv)):
            remote(b_sb.at[i, 2, side], b_rb.at[i, 2, side], ss_b.at[i, 2, side],
                   rs_b.at[i, 2, side], {"head": where}).wait_recv()
        proj = part[i, y] + b_rb[i, 2, 0].astype(F32) + b_rb[i, 2, 1].astype(F32)
        part[i, y] = proj
        al = aligned[rows_of(i), :]
        pp = jnp.sum(proj * proj, axis=1, keepdims=True)
        pa = jnp.sum(proj * al, axis=1, keepdims=True)
        aa = jnp.sum(al * al, axis=1, keepdims=True)
        packed = jnp.where(lane == 0, fill(pp), jnp.where(lane == 1, fill(pa), jnp.where(lane == 2, fill(aa), 0.0)))
        stat[i, ec] = packed.T[0:8, :]
        for d in range(1, 4):
            to = th * 4 + (ec + d) % 4
            go(remote(stat.at[i, ec], stat.at[i, ec], ss_st.at[i, d], rs_st.at[i, 4 - d], {"head": to}))
    for i in range(PHASES):
        for d in range(1, 4):
            fr = (ec + d) % 4
            remote(stat.at[i, fr], stat.at[i, fr], ss_st.at[i, d], rs_st.at[i, d], {"head": th * 4 + fr}).wait_recv()
        total = stat[i, 0] + stat[i, 1] + stat[i, 2] + stat[i, 3]
        pp, pa, aa = total[0:1], total[1:2], total[2:3]
        pn = jnp.sqrt(pp + cos_eps)
        an = jnp.sqrt(aa + cos_eps)
        cos = pa / (pn * an)
        first = 1.0 / (pn * an)
        second = cos / (pn * pn)
        cosx[0, i : i + 1, :] = cos
        cols = jnp.where(sub == 0, first, jnp.where(sub == 1, second, 0.0)).T
        al = aligned[rows_of(i), :]
        gp[i, y] = (-(al * cols[:SUB, 0:1] - cols[:SUB, 1:2] * part[i, y])).astype(BF)
        for side, where in ((0, nxt), (1, prv)):
            go(remote(gp.at[i, y], gp.at[i, y], ss_g.at[i, side], rs_g.at[i, side], {"head": where}))
    go(remote(cosx.at[0], cosx.at[1], ss_c.at[0], rs_c.at[0], {"head": (y + 4) % 8}))

    for s in range(1, 3):
        for i in range(PHASES):
            for side, where in ((0, nxt), (1, prv)):
                src = (y + 8 - s) % 8 if side == 0 else (y + s) % 8
                n = 2 * (s - 1) + side
                remote(gp.at[i, src], gp.at[i, src], ss_g.at[i, n], rs_g.at[i, n], {"head": where}).wait_recv()
                go(remote(gp.at[i, src], gp.at[i, src], ss_g.at[i, n + 2], rs_g.at[i, n + 2], {"head": where}))
    for i in range(PHASES):
        for side, where in ((0, nxt), (1, prv)):
            src = (y + 5) % 8 if side == 0 else (y + 3) % 8
            n = 4 + side
            remote(gp.at[i, src], gp.at[i, src], ss_g.at[i, n], rs_g.at[i, n], {"head": where}).wait_recv()
        src = (y + 3 + 2 * odd) % 8
        go(remote(gp.at[i, src], gp.at[i, src], ss_g.at[i, 6], rs_g.at[i, 6], {"head": buddy_of(y, 1 - odd)}))
    for i in range(PHASES):
        src = (y + 4) % 8
        remote(gp.at[i, src], gp.at[i, src], ss_g.at[i, 6], rs_g.at[i, 6], {"head": nxt}).wait_recv()

    full = jnp.concatenate(
        [
            jnp.concatenate([gp[i, t * 4 + e] for e in range(4)], axis=1)
            for t in range(2)
            for i in range(PHASES)
        ],
        axis=0,
    )
    attn_v = attn[...]
    grad = lax.dot_general(full, attn_v, (((0,), (0,)), ((), ())), preferred_element_type=F32)
    for xx in range(4):
        for zz in range(2):
            own[xx, zz] = grad[xx * EC + zz * 192 : xx * EC + (zz + 1) * 192]
    for xx in range(4):
        r1s[xx] = own[xx, o].astype(BF)
        go(remote(r1s.at[xx], r1r.at[xx], ss_r.at[xx], rs_r.at[xx], at_sib))
    grad_attn[...] = jnp.dot(full, w[...], preferred_element_type=F32).astype(BF)
    for xx in range(4):
        remote(r1s.at[xx], r1r.at[xx], ss_r.at[xx], rs_r.at[xx], at_sib).wait_recv()
    far = own[xo, c] + r1r[xo].astype(F32)
    r2h[0] = far[:96].astype(BF)
    r2h[1] = far[96:].astype(BF)
    go(remote(r2h.at[0], r2h.at[2], ss_r.at[4], rs_r.at[4], at_xu))
    go(remote(r2h.at[1], r2h.at[3], ss_r.at[5], rs_r.at[5], at_xd))
    near_u = own[xu, c] + r1r[xu].astype(F32)
    near_d = own[xd, c] + r1r[xd].astype(F32)
    r2s[0, 96:] = near_u[96:].astype(BF)
    r2s[1, :96] = near_d[:96].astype(BF)
    mine = own[x, c] + r1r[x].astype(F32)
    remote(r2h.at[0], r2h.at[2], ss_r.at[4], rs_r.at[4], at_xu).wait_recv()
    r2s[0, :96] = (near_u[:96] + r2h[2].astype(F32)).astype(BF)
    go(remote(r2s.at[0], r2r.at[0], ss_r.at[6], rs_r.at[6], at_xu))
    remote(r2h.at[1], r2h.at[3], ss_r.at[5], rs_r.at[5], at_xd).wait_recv()
    r2s[1, 96:] = (near_d[96:] + r2h[3].astype(F32)).astype(BF)
    go(remote(r2s.at[1], r2r.at[1], ss_r.at[7], rs_r.at[7], at_xd))
    remote(r2s.at[0], r2r.at[0], ss_r.at[6], rs_r.at[6], at_xu).wait_recv()
    remote(r2s.at[1], r2r.at[1], ss_r.at[7], rs_r.at[7], at_xd).wait_recv()
    mine = mine + r2r[0].astype(F32) + r2r[1].astype(F32)

    for n in range(4):
        r3s[n] = mine[n * SUB : (n + 1) * SUB].astype(BF)
    pos = zh * 2 + zl
    for d in range(1, 8):
        to = (pos + d) % 8
        copy = remote(r3s.at[to // 2], r3r.at[d], ss_z.at[d], rs_z.at[d],
                      {"dp": x * 2 + to % 2, "seq": to // 2 * 2 + c})

        @pl.when(to % 2 == c)
        def _(copy=copy):
            copy.start()

    @pl.when(zl == c)
    def _():
        acc = r3s[zh].astype(F32)
        for d in range(1, 8):
            remote(r3s.at[0], r3r.at[d], ss_z.at[d], rs_z.at[d], at_sib).wait_recv()
            acc = acc + r3r[d].astype(F32)
        r4s[0] = acc[:24]
        r4s[1] = acc[24:]
        copy = remote(r4s.at[o], r4s.at[2], ss_r.at[8], rs_r.at[8], at_sib)
        copy.start()
        grad_proj[...] = r4s[c]
        copy.wait_send()

    remote(cosx.at[0], cosx.at[1], ss_c.at[0], rs_c.at[0], {"head": (y + 4) % 8}).wait_recv()
    row = jnp.zeros((8, 384), F32)
    token = lax.broadcasted_iota(jnp.int32, (8, 384), 1)
    for n in range(2):
        start = (th + (1 - 2 * th) * n) * HALF
        for i in range(PHASES):
            wide = jnp.concatenate(
                [jnp.broadcast_to(cosx[n, i : i + 1, :], (8, 128)), jnp.zeros((8, 256), F32)], axis=1
            )
            moved = pltpu.roll(wide, start + i * SUB, 1)
            row = jnp.where((token >= start + i * SUB) & (token < start + (i + 1) * SUB), moved, row)
    cos_out[...] = row[0:1, :TOK]

    @pl.when(zl != c)
    def _():
        remote(r4s.at[0], r4s.at[2], ss_r.at[8], rs_r.at[8], at_sib).wait_recv()
        grad_proj[...] = r4s[2]

    for d in range(1, 8):
        to = (pos + d) % 8
        copy = remote(r3s.at[to // 2], r3r.at[d], ss_z.at[d], rs_z.at[d],
                      {"dp": x * 2 + to % 2, "seq": to // 2 * 2 + c})

        @pl.when(to % 2 == c)
        def _(copy=copy):
            copy.wait_send()

    for copy in sent:
        copy.wait_send()


def buddy_of(y, odd):
    return (y + 1 + 6 * odd) % 8


def on_device(patch_in, enc_weight, enc_gain, enc_bias, interp_index, queries, key_rows, value_rows, proj_weight):
    vm = pl.BlockSpec(memory_space=pltpu.VMEM)
    dma = pltpu.SemaphoreType.DMA
    attn, aligned = pl.pallas_call(
        front,
        out_shape=(jax.ShapeDtypeStruct((TOK, DA), BF), jax.ShapeDtypeStruct((TOK, EC), F32)),
        in_specs=[vm] * 8,
        out_specs=(vm, vm),
        scratch_shapes=[
            pltpu.VMEM((NH, 8, TOK, HD), BF),
            pltpu.VMEM((NH, 8, TOK, HD), BF),
            pltpu.VMEM((4, 2, 16, E), F32),
            pltpu.VMEM((4, 16, E), F32),
            pltpu.VMEM((2, 16, E // 2), BF),
            pltpu.VMEM((2, 16, E // 2), BF),
            pltpu.VMEM((2, 16, E), BF),
            pltpu.VMEM((2, 16, E), BF),
            pltpu.VMEM((4, 16, EC), BF),
            pltpu.VMEM((8, 8, 16, EC), BF),
            dma((NH, 7)),
            dma((NH, 8)),
            dma((NH, 7)),
            dma((NH, 8)),
            dma((8,)),
            dma((8,)),
            dma((8,)),
            dma((8,)),
            dma((8,)),
            dma((9,)),
        ],
        compiler_params=pltpu.CompilerParams(
            collective_id=0, has_side_effects=True, vmem_limit_bytes=48 * 2**20
        ),
        name="front",
    )(
        patch_in[0],
        enc_weight,
        enc_gain,
        enc_bias,
        interp_index,
        queries[0],
        key_rows[0],
        value_rows[0],
    )
    cosine, grad_attn, grad_proj = pl.pallas_call(
        tail,
        out_shape=(
            jax.ShapeDtypeStruct((1, TOK), F32),
            jax.ShapeDtypeStruct((TOK, DA), BF),
            jax.ShapeDtypeStruct((24, DA), F32),
        ),
        in_specs=[vm] * 3,
        out_specs=(vm, vm, vm),
        scratch_shapes=[
            pltpu.VMEM((PHASES, 8, SUB, EC), F32),
            pltpu.VMEM((PHASES, SUB, EC), BF),
            pltpu.VMEM((PHASES, SUB, EC), BF),
            pltpu.VMEM((PHASES, 3, 2, SUB, EC), BF),
            pltpu.VMEM((PHASES, 3, 2, SUB, EC), BF),
            pltpu.VMEM((PHASES, 4, 8, 128), F32),
            pltpu.VMEM((2, 8, 128), F32),
            pltpu.VMEM((PHASES, 8, SUB, EC), BF),
            pltpu.VMEM((4, 192, DA), BF),
            pltpu.VMEM((4, 192, DA), BF),
            pltpu.VMEM((4, 2, 192, DA), F32),
            pltpu.VMEM((2, 192, DA), BF),
            pltpu.VMEM((2, 192, DA), BF),
            pltpu.VMEM((4, 96, DA), BF),
            pltpu.VMEM((4, SUB, DA), BF),
            pltpu.VMEM((8, SUB, DA), BF),
            pltpu.VMEM((3, 24, DA), F32),
            dma((PHASES,)),
            dma((PHASES,)),
            dma((PHASES, 3, 2)),
            dma((PHASES, 3, 2)),
            dma((PHASES, 4)),
            dma((PHASES, 4)),
            dma((1,)),
            dma((1,)),
            dma((PHASES, 7)),
            dma((PHASES, 7)),
            dma((9,)),
            dma((9,)),
            dma((8,)),
            dma((8,)),
        ],
        compiler_params=pltpu.CompilerParams(
            collective_id=1, has_side_effects=True, vmem_limit_bytes=48 * 2**20
        ),
        name="tail",
    )(attn, proj_weight, aligned)
    return attn[None], cosine, grad_attn[None], grad_proj


def solution(mesh):
    placed = (
        P("dp", "head", "seq"),
        P("seq", None),
        P(),
        P(),
        P("dp", "seq"),
        P("dp", "seq", "head"),
        P("dp", "seq", "head"),
        P("dp", "seq", "head"),
        P(None, "head"),
    )
    return jax.shard_map(
        on_device,
        mesh=mesh,
        in_specs=placed,
        out_specs=(
            P("dp", "seq", "head"),
            P("dp", "seq"),
            P("dp", "seq", "head"),
            P(("dp", "seq"), "head"),
        ),
        check_vma=False,
    )
```

```python
import jax
import jax.numpy as jnp
from jax import lax
from jax.experimental import pallas as pl
from jax.experimental.pallas import tpu as pltpu
from jax.sharding import PartitionSpec as P

MESH = pl.DeviceIdType.MESH
BF = jnp.bfloat16
F32 = jnp.float32

E = 1536
HD = 128
NH = 3
DA = NH * HD
TOK = 288
SUB = 48
EC = 384
PH = 3
PT = 2 * SUB
BLK = 192

layer_eps = 1e-06
cos_eps = 1e-06
EXP_SCALE = HD**-0.5 * 1.4426950408889634


def remote(src, dst, send, recv, where):
    return pltpu.make_async_remote_copy(
        src_ref=src, dst_ref=dst, send_sem=send, recv_sem=recv, device_id=where, device_id_type=MESH
    )


def kernel(
    patch_h, enc_h, gain_h, bias_h, idx_h, q_h, k_h, v_h, w_h,
    attn, cos_out, grad_attn, grad_proj,
    patch, enc_w, gain, bias, idx, w, q3, k3, v3,
    qb, kb, vb, ob, at3, part, e1r, e2s, e2r, tn, tb, aligned,
    pp, s1, r1, sf, rf, s2, r2, pr, stat, cosx,
    own, g1s, g1r, g2s, g2r, g3s, g3r,
    l_s, l3_s, k_s, k_r, ks_s, ks_r, v_s, v_r, vs_s, vs_r, q_s, q_r, o_s, o_r, e_s, e_r, t_s, t_r, ty_s, ty_r, tc_s, tc_r,
    p_s, p_r, st_s, st_r, c_s, c_r, a_s, a_r, g_s, g_r, z_s, z_r,
):
    dp, seq, y = lax.axis_index("dp"), lax.axis_index("seq"), lax.axis_index("head")
    x, zl, zh, c = dp // 2, dp % 2, seq // 2, seq % 2
    o = 1 - c
    odd = y % 2
    half, chunk = y // 4, y % 4
    pos = zh * 2 + zl
    at_sib = {"seq": zh * 2 + o}
    sent = []

    def at_y(d):
        return {"head": (y + d) % 8}

    def go(copy):
        copy.start()
        sent.append(copy)

    loads = [
        pltpu.make_async_copy(src, dst, l_s.at[n])
        for n, (src, dst) in enumerate(
            ((patch_h, patch), (enc_h, enc_w), (gain_h, gain), (bias_h, bias), (idx_h, idx), (w_h, w))
        )
    ]
    qkv_loads = [
        [
            pltpu.make_async_copy(src.at[:, h * HD : (h + 1) * HD], dst.at[h], l3_s.at[n, h])
            for h in range(NH)
        ]
        for n, (src, dst) in enumerate(((k_h, k3), (v_h, v3), (q_h, q3)))
    ]
    for copy in (*loads[:2], *qkv_loads[0], *qkv_loads[1], *qkv_loads[2], *loads[2:]):
        copy.start()

    barrier = pltpu.get_barrier_semaphore()
    peers = [at_y(d) for d in range(1, 8)]
    peers += [{"dp": (x + d) % 4 * 2 + zl} for d in (1, 2, 3)]
    peers += [at_sib]
    for d in range(1, 8):
        to = (pos + d) % 8
        for cc in range(2):
            peers.append({"dp": x * 2 + to % 2, "seq": to // 2 * 2 + cc})
    for peer in peers:
        pl.semaphore_signal(barrier, inc=1, device_id=peer, device_id_type=MESH)
    pl.semaphore_wait(barrier, len(peers))

    first = 2 * zl + 1
    mine_r = (zh + 4 - first) % 4
    active = mine_r < NH
    workers = [(first + r) % 4 for r in range(NH)]
    cond_sent = []

    def go_if(cond, copy):
        cond_sent.append((cond, copy))

        @pl.when(cond)
        def _():
            copy.start()

    def scatter(src, buf, ss, rs):
        for r, worker in enumerate(workers):
            go_if(worker != zh, remote(src.at[r], buf.at[seq], ss.at[r], rs.at[zh], {"seq": worker * 2 + c}))

    def to_sib(buf, ss, rs, z):
        copy = remote(buf.at[z * 2 + c], buf.at[z * 2 + c], ss.at[z], rs.at[z], at_sib)
        copy.start()
        return copy

    def keep(src, buf, ss, rs):
        @pl.when(active)
        def _():
            buf[seq] = src[mine_r]
            to_sib(buf, ss, rs, zh)

    def pass_on(buf, rs, ss2, rs2):
        @pl.when(active)
        def _():
            for d in (1, 3, 2):
                z = (zh + d) % 4
                remote(buf.at[z * 2 + c], buf.at[z * 2 + c], rs.at[z], rs.at[z], at_sib).wait_recv()
                to_sib(buf, ss2, rs2, z)

    loads[0].wait()
    loads[1].wait()
    share = lax.dot_general(
        patch[...], enc_w[...], (((0,), (0,)), ((), ())), preferred_element_type=F32
    )
    for z in range(4):
        for cc in range(2):
            part[cc, z] = share[(2 * z + cc) * 16 : (2 * z + cc + 1) * 16]
    e1 = remote(part.at[o], e1r, e_s.at[0], e_r.at[0], at_sib)
    go(e1)
    for copy in qkv_loads[0]:
        copy.wait()
    scatter(k3, kb, k_s, k_r)
    keep(k3, kb, ks_s, ks_r)
    e1.wait_recv()
    for d in (2, 1, 3):
        to = (zh + d) % 4
        e2s[d] = (part[c, to] + e1r[to]).astype(BF)
        go(remote(e2s.at[d], e2r.at[4 - d], e_s.at[d], e_r.at[4 - d], {"seq": to * 2 + c}))
    for copy in qkv_loads[1]:
        copy.wait()
    scatter(v3, vb, v_s, v_r)
    keep(v3, vb, vs_s, vs_r)
    enc = part[c, zh] + e1r[zh]
    for d in (1, 2, 3):
        remote(e2s.at[d], e2r.at[d], e_s.at[d], e_r.at[d], at_sib).wait_recv()
        enc = enc + e2r[d].astype(F32)
    loads[2].wait()
    loads[3].wait()
    average = jnp.mean(enc, axis=1, keepdims=True)
    centred = enc - average
    variance = jnp.mean(centred * centred, axis=1, keepdims=True)
    normed = (
        centred * lax.rsqrt(variance + layer_eps) * gain[...].reshape(1, E) + bias[...].reshape(1, E)
    ).astype(BF)
    for e in range(4):
        tn[e, zh] = normed[:, e * EC : (e + 1) * EC]
    for d in (2, 1, 3):
        to = (zh + d) % 4
        go(remote(tn.at[:, zh], tn.at[:, zh], t_s.at[d], t_r.at[4 - d], {"seq": to * 2 + c}))
    for copy in qkv_loads[2]:
        copy.wait()
    for i in range(PH):
        rows = slice(i * PT, (i + 1) * PT)
        for r, worker in enumerate(workers):
            go_if(
                worker != zh,
                remote(q3.at[r, rows], qb.at[i, zh], q_s.at[i, r], q_r.at[i, zh], {"seq": worker * 2 + c}),
            )
    pass_on(kb, k_r, ks_s, ks_r)
    for d in (1, 2, 3):
        fr = (zh + d) % 4
        remote(tn.at[:, fr], tn.at[:, fr], t_s.at[d], t_r.at[d], at_sib).wait_recv()
    for d in (4, 3, 5, 2, 6, 1, 7):
        go(remote(tn.at[(y + d) % 4], tb.at[y, c], ty_s.at[d], ty_r.at[8 - d], at_y(d)))
    tb[y, c] = tn[chunk]

    def gather_start(at, ss, rs):
        for n, d in enumerate((2, 6, 1, 7)):
            go(remote(at(y), at(y), ss(n), rs(8 - d), at_y(d)))

    def gather_took(at, rs, d):
        fr = (y + d) % 8
        remote(at(fr), at(fr), rs(d), rs(d), at_y(d)).wait_recv()

    def gather_relay(at, ss, rs):
        gather_took(at, rs, 6)
        lo = (y + 6) % 8
        gather_took(at, rs, 2)
        hi = (y + 2) % 8
        far = (y + 6 + 4 * odd) % 8
        go(remote(at(far), at(far), ss(6), rs(4), at_y(2 + 4 * odd)))
        go(remote(at(lo), at(lo), ss(4), rs(5), at_y(1)))
        go(remote(at(hi), at(hi), ss(5), rs(3), at_y(7)))

    pass_on(vb, v_r, vs_s, vs_r)

    @pl.when(active)
    def _():
        for buf, rs in ((kb, ks_r), (vb, vs_r)):
            for z in range(4):
                remote(buf.at[z * 2 + o], buf.at[z * 2 + o], rs.at[z], rs.at[z], at_sib).wait_recv()
        for i in range(PH):
            rows = slice(i * PT, (i + 1) * PT)
            qb[i, zh] = q3[mine_r, rows]
            for d in (1, 3, 2):
                z = (zh + d) % 4
                remote(qb.at[i, z], qb.at[i, z], q_r.at[i, z], q_r.at[i, z], at_sib).wait_recv()
            scores = lax.dot_general(
                qb[i].reshape(4 * PT, HD), kb[...].reshape(8 * TOK, HD), (((1,), (1,)), ((), ())),
                preferred_element_type=F32,
            )
            top = jnp.max(scores, axis=1, keepdims=True)
            expo = jnp.exp2((scores - top) * EXP_SCALE).astype(BF)
            wide = jnp.concatenate([vb[...].reshape(8 * TOK, HD), jnp.ones((8 * TOK, HD), BF)], axis=1)
            out = jnp.dot(expo, wide, preferred_element_type=F32)
            ob[i] = (out[:, :HD] / out[:, HD:]).astype(BF).reshape(4, PT, HD)
            for d in (2, 1, 3):
                z = (zh + d) % 4
                remote(ob.at[i, z], at3.at[mine_r, rows], o_s.at[i, d], o_r.at[mine_r, i], {"seq": z * 2 + c}).start()
            at3[mine_r, rows] = ob[i, zh]

    loads[5].wait()

    for i in range(PH):
        rows = slice(i * PT, (i + 1) * PT)
        for r, worker in enumerate(workers):

            @pl.when(worker != zh)
            def _(r=r, rows=rows, i=i):
                remote(at3.at[r, rows], at3.at[r, rows], o_r.at[r, i], o_r.at[r, i], at_sib).wait_recv()

        attn[rows, :] = jnp.concatenate([at3[r, rows] for r in range(NH)], axis=1)
        partial = lax.dot_general(
            attn[rows, :], w[...], (((1,), (1,)), ((), ())), preferred_element_type=F32
        )
        for t in range(2):
            for e in range(4):
                pp[i, t * 4 + e] = partial[t * SUB : (t + 1) * SUB, e * EC : (e + 1) * EC]
        sf[i] = pp[i, (y + 4) % 8].astype(BF)
        go(remote(sf.at[i], rf.at[i], p_s.at[i, 0], p_r.at[i, 0], at_y(2 + 4 * odd)))
        s1[i, 0, 1] = pp[i, (y + 3) % 8].astype(BF)
        s1[i, 0, 0] = pp[i, (y + 1) % 8].astype(BF)
        go(remote(s1.at[i, 0], r1.at[i, 0], p_s.at[i, 1], p_r.at[i, 1], at_y(1)))
        s1[i, 1, 1] = pp[i, (y + 5) % 8].astype(BF)
        s1[i, 1, 0] = pp[i, (y + 7) % 8].astype(BF)
        go(remote(s1.at[i, 1], r1.at[i, 1], p_s.at[i, 2], p_r.at[i, 2], at_y(7)))
    for d in range(1, 8):
        fr = (y + d) % 8
        remote(tb.at[fr, c], tb.at[fr, c], ty_s.at[d], ty_r.at[d], at_y(d)).wait_recv()
    to_core = remote(tb.at[:, c], tb.at[:, c], tc_s.at[0], tc_r.at[0], at_sib)
    go(to_core)
    for i in range(PH):
        remote(sf.at[i], rf.at[i], p_s.at[i, 0], p_r.at[i, 0], at_y(1)).wait_recv()
        remote(s1.at[i, 0], r1.at[i, 0], p_s.at[i, 1], p_r.at[i, 1], at_y(1)).wait_recv()
        remote(s1.at[i, 1], r1.at[i, 1], p_s.at[i, 2], p_r.at[i, 2], at_y(7)).wait_recv()
        far = rf[i].astype(F32)
        upper = pp[i, (y + 2) % 8] + r1[i, 0, 1].astype(F32)
        lower = pp[i, (y + 6) % 8] + r1[i, 1, 1].astype(F32)
        s2[i, 0] = jnp.where(odd == 0, upper + far, upper).astype(BF)
        go(remote(s2.at[i, 0], r2.at[i, 0], p_s.at[i, 3], p_r.at[i, 3], at_y(2)))
        s2[i, 1] = jnp.where(odd == 1, lower + far, lower).astype(BF)
        go(remote(s2.at[i, 1], r2.at[i, 1], p_s.at[i, 4], p_r.at[i, 4], at_y(6)))

    loads[4].wait()
    picks = idx[...]
    rest = picks % 128
    spot = picks // 128 * 128 + rest // 16 % 2 * 64 + rest // 32 * 16 + rest % 16
    hot = (lax.broadcasted_iota(jnp.int32, (1024, TOK), 0) == spot).astype(F32).astype(BF)
    remote(tb.at[:, o], tb.at[:, o], tc_s.at[0], tc_r.at[0], at_sib).wait_recv()
    aligned[...] = lax.dot_general(
        hot, tb[...].reshape(1024, EC), (((0,), (0,)), ((), ())), preferred_element_type=F32
    )

    lane = lax.broadcasted_iota(jnp.int32, (128, 128), 1)
    sub = lax.broadcasted_iota(jnp.int32, (128, 128), 0)

    def tall(column):
        return jnp.concatenate([column, jnp.zeros((128 - SUB, 1), F32)], axis=0)

    def own_rows(i):
        return pl.ds(pl.multiple_of(i * PT + half * SUB, 16), SUB)

    for i in range(PH):
        remote(s2.at[i, 0], r2.at[i, 0], p_s.at[i, 3], p_r.at[i, 3], at_y(2)).wait_recv()
        remote(s2.at[i, 1], r2.at[i, 1], p_s.at[i, 4], p_r.at[i, 4], at_y(6)).wait_recv()
        proj = (
            pp[i, y]
            + (r1[i, 0, 0].astype(F32) + r1[i, 1, 0].astype(F32))
            + (r2[i, 0].astype(F32) + r2[i, 1].astype(F32))
        )
        pp[i, y] = proj
        al = aligned[own_rows(i), :]
        sums = [jnp.sum(v, axis=1, keepdims=True) for v in (proj * proj, proj * al, al * al)]
        packed = jnp.where(
            lane == 0, tall(sums[0]), jnp.where(lane == 1, tall(sums[1]), jnp.where(lane == 2, tall(sums[2]), 0.0))
        )
        stat[i, chunk] = packed.T[0:8, :]
        for d in (2, 1, 3):
            to = half * 4 + (chunk + d) % 4
            go(remote(stat.at[i, chunk], stat.at[i, chunk], st_s.at[i, d], st_r.at[i, 4 - d], {"head": to}))

    def grad_at(i):
        return (lambda n: pr.at[i, n]), (lambda n: a_s.at[i, n]), (lambda n: a_r.at[i, n])

    for i in range(PH):
        for d in (1, 2, 3):
            fr = (chunk + d) % 4
            remote(stat.at[i, fr], stat.at[i, fr], st_s.at[i, d], st_r.at[i, d], at_sib).wait_recv()
        total = (stat[i, 0] + stat[i, 1]) + (stat[i, 2] + stat[i, 3])
        pn = jnp.sqrt(total[0:1] + cos_eps)
        an = jnp.sqrt(total[2:3] + cos_eps)
        cos = total[1:2] / (pn * an)
        cosx[0, i] = jnp.broadcast_to(cos, (8, 128))
        factors = jnp.where(sub == 0, 1.0 / (pn * an), jnp.where(sub == 1, cos / (pn * pn), 0.0)).T
        al = aligned[own_rows(i), :]
        pr[i, y] = (-(al * factors[:SUB, 0:1] - factors[:SUB, 1:2] * pp[i, y])).astype(BF)
        gather_start(*grad_at(i))
    go(remote(cosx.at[0], cosx.at[1], c_s.at[0], c_r.at[0], at_y(4)))
    for i in range(PH):
        gather_relay(*grad_at(i))
    for i in range(PH):
        at, ss, rs = grad_at(i)
        for d in (1, 7, 3, 5, 4):
            gather_took(at, rs, d)

    def grad_columns(e):
        return jnp.concatenate([pr[i, t * 4 + e] for i in range(PH) for t in range(2)], axis=0)

    xo, xu, xd = (x + 2) % 4, (x + 1) % 4, (x + 3) % 4
    for n, xx in enumerate((xo, xu, xd, x)):
        block = lax.dot_general(grad_columns(xx), attn[...], (((0,), (0,)), ((), ())), preferred_element_type=F32)
        for zz in range(2):
            own[xx, zz] = block[zz * BLK : (zz + 1) * BLK]
        g1s[n] = own[xx, o].astype(BF)
        go(remote(g1s.at[n], g1r.at[n], g_s.at[n], g_r.at[n], at_sib))
    for n, (xx, d) in enumerate(((xo, 2), (xu, 1), (xd, 3))):
        remote(g1s.at[n], g1r.at[n], g_s.at[n], g_r.at[n], at_sib).wait_recv()
        g2s[n] = (own[xx, c] + g1r[n].astype(F32)).astype(BF)
        go(remote(g2s.at[n], g2r.at[4 - d], g_s.at[3 + d], g_r.at[8 - d], {"dp": xx * 2 + zl}))
    back = jnp.dot(grad_columns(0), w[:EC], preferred_element_type=F32)
    for e in range(1, 4):
        back = back + jnp.dot(grad_columns(e), w[e * EC : (e + 1) * EC], preferred_element_type=F32)
    grad_attn[...] = back.astype(BF)
    remote(g1s.at[3], g1r.at[3], g_s.at[3], g_r.at[3], at_sib).wait_recv()
    mine = own[x, c] + g1r[3].astype(F32)
    for d in (1, 3, 2):
        remote(g2s.at[0], g2r.at[d], g_s.at[3 + d], g_r.at[4 + d], {"dp": xu * 2 + zl}).wait_recv()
        mine = mine + g2r[d].astype(F32)
    for n in range(8):
        g3s[n] = jnp.concatenate([mine[n * 24 : (n + 1) * 24], jnp.zeros((8, DA), F32)], axis=0).astype(BF)
    z_sends = []
    for dz in range(4):
        for cc in range(2):
            to = (zh + dz) % 4
            copy = remote(g3s.at[to * 2 + cc], g3r.at[pos], z_s.at[dz, cc], z_r.at[pos],
                          {"dp": x * 2 + c, "seq": to * 2 + cc})
            if dz == 0:
                away = (zl != c) | (c != cc)
                z_sends.append((copy, away))

                @pl.when(away)
                def _(copy=copy):
                    copy.start()
            else:
                go(copy)
    row = jnp.zeros((8, 384), F32)
    token = lax.broadcasted_iota(jnp.int32, (8, 384), 1)
    remote(cosx.at[0], cosx.at[1], c_s.at[0], c_r.at[0], at_y(4)).wait_recv()
    for n in range(2):
        for i in range(PH):
            start = i * PT + (half + (1 - 2 * half) * n) * SUB
            wide = jnp.concatenate([cosx[n, i], jnp.zeros((8, 256), F32)], axis=1)
            inside = (token >= start) & (token < start + SUB)
            row = jnp.where(inside, pltpu.roll(wide, start, 1), row)
    cos_out[...] = row[0:1, :TOK]

    @pl.when(zl == c)
    def _():
        g3r[pos] = g3s[zh * 2 + c]

    @pl.when(zl != c)
    def _():
        remote(g3s.at[0], g3r.at[pos], z_s.at[0, 0], z_r.at[pos], at_sib).wait_recv()

    for d in range(1, 8):
        fr = (pos + d) % 8
        remote(g3s.at[0], g3r.at[fr], z_s.at[0, 0], z_r.at[fr], at_sib).wait_recv()
    total = g3r[0].astype(F32)
    for n in range(1, 8):
        total = total + g3r[n].astype(F32)
    grad_proj[...] = total[:24]

    @pl.when(active)
    def _():
        for z in range(4):
            for buf, ss in ((kb, ks_s), (vb, vs_s)):
                remote(buf.at[z * 2 + c], buf.at[z * 2 + c], ss.at[z], ks_r.at[z], at_sib).wait_send()
        for i in range(PH):
            for d in (1, 2, 3):
                remote(ob.at[i, d], at3.at[0, :PT], o_s.at[i, d], o_r.at[0, i], at_sib).wait_send()

    for cond, copy in cond_sent:

        @pl.when(cond)
        def _(copy=copy):
            copy.wait_send()

    for copy, away in z_sends:

        @pl.when(away)
        def _(copy=copy):
            copy.wait_send()

    for copy in sent:
        copy.wait_send()


def settle(a, b, c, d, a_out, b_out, c_out, d_out, a_in, b_in, c_in, d_in, sems):
    first = [
        pltpu.make_async_copy(src, dst, sems.at[n])
        for n, (src, dst) in enumerate(((a, a_in), (b, b_in), (c, c_in), (d, d_in)))
    ]
    second = [
        pltpu.make_async_copy(src, dst, sems.at[n + 4])
        for n, (src, dst) in enumerate(((a_in, a_out), (b_in, b_out), (c_in, c_out), (d_in, d_out)))
    ]
    for copy in first:
        copy.start()
    for one, two in zip(first, second):
        one.wait()
        two.start()
    for copy in second:
        copy.wait()


def on_device(patch_in, enc_weight, enc_gain, enc_bias, interp_index, queries, key_rows, value_rows, proj_weight):
    vm = pl.BlockSpec(memory_space=pltpu.VMEM)
    hbm = pl.BlockSpec(memory_space=pltpu.HBM)
    dma = pltpu.SemaphoreType.DMA
    attn, cosine, grad_attn, grad_proj = pl.pallas_call(
        kernel,
        out_shape=(
            jax.ShapeDtypeStruct((TOK, DA), BF),
            jax.ShapeDtypeStruct((1, TOK), F32),
            jax.ShapeDtypeStruct((TOK, DA), BF),
            jax.ShapeDtypeStruct((24, DA), F32),
        ),
        in_specs=[hbm] * 9,
        out_specs=(vm,) * 4,
        scratch_shapes=[
            pltpu.VMEM((192, 128), BF),
            pltpu.VMEM((192, E), BF),
            pltpu.VMEM((E,), F32),
            pltpu.VMEM((E,), F32),
            pltpu.VMEM((1, TOK), jnp.int32),
            pltpu.VMEM((E, DA), BF),
            pltpu.VMEM((NH, TOK, HD), BF),
            pltpu.VMEM((NH, TOK, HD), BF),
            pltpu.VMEM((NH, TOK, HD), BF),
            pltpu.VMEM((PH, 4, PT, HD), BF),
            pltpu.VMEM((8, TOK, HD), BF),
            pltpu.VMEM((8, TOK, HD), BF),
            pltpu.VMEM((PH, 4, PT, HD), BF),
            pltpu.VMEM((NH, TOK, HD), BF),
            pltpu.VMEM((2, 4, 16, E), F32),
            pltpu.VMEM((4, 16, E), F32),
            pltpu.VMEM((4, 16, E), BF),
            pltpu.VMEM((4, 16, E), BF),
            pltpu.VMEM((4, 4, 16, EC), BF),
            pltpu.VMEM((8, 2, 4, 16, EC), BF),
            pltpu.VMEM((TOK, EC), F32),
            pltpu.VMEM((PH, 8, SUB, EC), F32),
            pltpu.VMEM((PH, 2, 2, SUB, EC), BF),
            pltpu.VMEM((PH, 2, 2, SUB, EC), BF),
            pltpu.VMEM((PH, SUB, EC), BF),
            pltpu.VMEM((PH, SUB, EC), BF),
            pltpu.VMEM((PH, 2, SUB, EC), BF),
            pltpu.VMEM((PH, 2, SUB, EC), BF),
            pltpu.VMEM((PH, 8, SUB, EC), BF),
            pltpu.VMEM((PH, 4, 8, 128), F32),
            pltpu.VMEM((2, PH, 8, 128), F32),
            pltpu.VMEM((4, 2, BLK, DA), F32),
            pltpu.VMEM((4, BLK, DA), BF),
            pltpu.VMEM((4, BLK, DA), BF),
            pltpu.VMEM((3, BLK, DA), BF),
            pltpu.VMEM((4, BLK, DA), BF),
            pltpu.VMEM((8, 32, DA), BF),
            pltpu.VMEM((8, 32, DA), BF),
            dma((6,)),
            dma((3, NH)),
            dma((NH,)),
            dma((4,)),
            dma((4,)),
            dma((4,)),
            dma((NH,)),
            dma((4,)),
            dma((4,)),
            dma((4,)),
            dma((PH, NH)),
            dma((PH, 4)),
            dma((PH, 4)),
            dma((NH, PH)),
            dma((4,)),
            dma((4,)),
            dma((4,)),
            dma((4,)),
            dma((8,)),
            dma((8,)),
            dma((8,)),
            dma((8,)),
            dma((PH, 5)),
            dma((PH, 5)),
            dma((PH, 4)),
            dma((PH, 4)),
            dma((1,)),
            dma((1,)),
            dma((PH, 8)),
            dma((PH, 8)),
            dma((8,)),
            dma((8,)),
            dma((4, 2)),
            dma((8,)),
        ],
        compiler_params=pltpu.CompilerParams(
            collective_id=0, has_side_effects=True, vmem_limit_bytes=56 * 2**20
        ),
        name="whole",
    )(
        patch_in[0].T,
        enc_weight,
        enc_gain,
        enc_bias,
        interp_index,
        queries[0],
        key_rows[0],
        value_rows[0],
        proj_weight,
    )
    results = (attn, cosine, grad_attn, grad_proj)
    attn, cosine, grad_attn, grad_proj = pl.pallas_call(
        settle,
        out_shape=tuple(jax.ShapeDtypeStruct(a.shape, a.dtype) for a in results),
        in_specs=[hbm] * 4,
        out_specs=(hbm,) * 4,
        scratch_shapes=[pltpu.VMEM(a.shape, a.dtype) for a in results] + [dma((8,))],
        compiler_params=pltpu.CompilerParams(vmem_limit_bytes=60 * 2**20),
        name="settle",
    )(*results)
    return attn[None], cosine, grad_attn[None], grad_proj


def solution(mesh):
    placed = (
        P("dp", "head", "seq"),
        P("seq", None),
        P(),
        P(),
        P("dp", "seq"),
        P("dp", "seq", "head"),
        P("dp", "seq", "head"),
        P("dp", "seq", "head"),
        P(None, "head"),
    )
    return jax.shard_map(
        on_device,
        mesh=mesh,
        in_specs=placed,
        out_specs=(
            P("dp", "seq", "head"),
            P("dp", "seq"),
            P("dp", "seq", "head"),
            P(("dp", "seq"), "head"),
        ),
        check_vma=False,
    )
```

```python
import jax
import jax.numpy as jnp
from jax import lax
from jax.experimental import pallas as pl
from jax.experimental.pallas import tpu as pltpu
from jax.sharding import PartitionSpec as P

MESH = pl.DeviceIdType.MESH
BF = jnp.bfloat16
F32 = jnp.float32

E = 1536
HD = 128
NH = 3
DA = NH * HD
TOK = 288
SUB = 48
EC = 384
PH = 3
PT = 2 * SUB
HB = 96
BLK = 192

layer_eps = 1e-06
cos_eps = 1e-06
EXP_SCALE = HD**-0.5 * 1.4426950408889634


def remote(src, dst, send, recv, where):
    return pltpu.make_async_remote_copy(
        src_ref=src, dst_ref=dst, send_sem=send, recv_sem=recv, device_id=where, device_id_type=MESH
    )


def kernel(
    patch_h, enc_h, gain_h, bias_h, idx_h, q_h, k_h, v_h, w_h,
    attn, cos_out, grad_attn, grad_proj,
    patch, enc_w, gain, bias, idx, w, q3, k3, v3,
    qb, kb, vb, ob, at3, part, e1r, e2s, e2r, tn, tb, aligned,
    pp, s1, r1, sf, rf, s2, r2, pr, stat, cosx,
    own, g1s, g1r, g2s, g2r, g3s, g3r,
    l_s, l3_s, k_s, k_r, ks_s, ks_r, v_s, v_r, vs_s, vs_r, q_s, q_r, o_s, o_r, e_s, e_r, t_s, t_r, ty_s, ty_r, tc_s, tc_r,
    p_s, p_r, st_s, st_r, c_s, c_r, a_s, a_r, g_s, g_r, x_s, x_r, z_s, z_r,
):
    dp, seq, y = lax.axis_index("dp"), lax.axis_index("seq"), lax.axis_index("head")
    x, zl, zh, c = dp // 2, dp % 2, seq // 2, seq % 2
    o = 1 - c
    odd = y % 2
    half, chunk = y // 4, y % 4
    pos = zh * 2 + zl
    at_sib = {"seq": zh * 2 + o}
    sent = []

    def at_y(d):
        return {"head": (y + d) % 8}

    def go(copy):
        copy.start()
        sent.append(copy)

    loads = [
        pltpu.make_async_copy(src, dst, l_s.at[n])
        for n, (src, dst) in enumerate(
            ((patch_h, patch), (enc_h, enc_w), (gain_h, gain), (bias_h, bias), (idx_h, idx), (w_h, w))
        )
    ]
    qkv_loads = [
        [
            pltpu.make_async_copy(src.at[:, h * HD : (h + 1) * HD], dst.at[h], l3_s.at[n, h])
            for h in range(NH)
        ]
        for n, (src, dst) in enumerate(((k_h, k3), (v_h, v3), (q_h, q3)))
    ]
    for copy in (*loads[:2], *qkv_loads[0], *qkv_loads[1], *qkv_loads[2], *loads[2:]):
        copy.start()

    barrier = pltpu.get_barrier_semaphore()
    peers = [at_y(d) for d in range(1, 8)]
    peers += [{"dp": (x + d) % 4 * 2 + zl} for d in (1, 2, 3)]
    peers += [at_sib]
    for d in range(1, 8):
        to = (pos + d) % 8
        for cc in range(2):
            peers.append({"dp": x * 2 + to % 2, "seq": to // 2 * 2 + cc})
    for peer in peers:
        pl.semaphore_signal(barrier, inc=1, device_id=peer, device_id_type=MESH)
    loads[0].wait()
    loads[1].wait()
    share = lax.dot_general(
        patch[...], enc_w[...], (((0,), (0,)), ((), ())), preferred_element_type=F32
    )
    for z in range(4):
        for cc in range(2):
            part[cc, z] = share[(2 * z + cc) * 16 : (2 * z + cc + 1) * 16]
    for group in qkv_loads:
        for copy in group:
            copy.wait()
    pl.semaphore_wait(barrier, len(peers))

    first = 2 * zl + 1
    mine_r = (zh + 4 - first) % 4
    active = mine_r < NH
    workers = [(first + r) % 4 for r in range(NH)]
    cond_sent = []

    def go_if(cond, copy):
        cond_sent.append((cond, copy))

        @pl.when(cond)
        def _():
            copy.start()

    def scatter(src, buf, ss, rs):
        for r, worker in enumerate(workers):
            go_if(worker != zh, remote(src.at[r], buf.at[seq], ss.at[r], rs.at[zh], {"seq": worker * 2 + c}))

    def to_sib(buf, ss, rs, z):
        copy = remote(buf.at[z * 2 + c], buf.at[z * 2 + c], ss.at[z], rs.at[z], at_sib)
        copy.start()
        return copy

    def keep(src, buf, ss, rs):
        @pl.when(active)
        def _():
            buf[seq] = src[mine_r]
            to_sib(buf, ss, rs, zh)

    def pass_on(buf, rs, ss2, rs2):
        @pl.when(active)
        def _():
            for d in (1, 3, 2):
                z = (zh + d) % 4
                remote(buf.at[z * 2 + c], buf.at[z * 2 + c], rs.at[z], rs.at[z], at_sib).wait_recv()
                to_sib(buf, ss2, rs2, z)

    scatter(k3, kb, k_s, k_r)
    scatter(v3, vb, v_s, v_r)
    for i in range(PH):
        rows = slice(i * PT, (i + 1) * PT)
        for r, worker in enumerate(workers):
            go_if(
                worker != zh,
                remote(q3.at[r, rows], qb.at[i, zh], q_s.at[i, r], q_r.at[i, zh], {"seq": worker * 2 + c}),
            )
    keep(k3, kb, ks_s, ks_r)
    keep(v3, vb, vs_s, vs_r)
    e1 = remote(part.at[o], e1r, e_s.at[0], e_r.at[0], at_sib)
    go(e1)
    e1.wait_recv()
    pass_on(kb, k_r, ks_s, ks_r)
    for d in (2, 1, 3):
        to = (zh + d) % 4
        e2s[d] = (part[c, to] + e1r[to]).astype(BF)
        go(remote(e2s.at[d], e2r.at[4 - d], e_s.at[d], e_r.at[4 - d], {"seq": to * 2 + c}))
    pass_on(vb, v_r, vs_s, vs_r)

    @pl.when(active)
    def _():
        for buf, rs in ((kb, ks_r), (vb, vs_r)):
            for z in range(4):
                remote(buf.at[z * 2 + o], buf.at[z * 2 + o], rs.at[z], rs.at[z], at_sib).wait_recv()

    def attend(i):
        rows = slice(i * PT, (i + 1) * PT)
        qb[i, zh] = q3[mine_r, rows]
        for d in (1, 3, 2):
            z = (zh + d) % 4
            remote(qb.at[i, z], qb.at[i, z], q_r.at[i, z], q_r.at[i, z], at_sib).wait_recv()
        scores = lax.dot_general(
            qb[i].reshape(4 * PT, HD), kb[...].reshape(8 * TOK, HD), (((1,), (1,)), ((), ())),
            preferred_element_type=F32,
        )
        top = jnp.max(scores, axis=1, keepdims=True)
        expo = jnp.exp2((scores - top) * EXP_SCALE).astype(BF)
        wide = jnp.concatenate([vb[...].reshape(8 * TOK, HD), jnp.ones((8 * TOK, HD), BF)], axis=1)
        out = jnp.dot(expo, wide, preferred_element_type=F32)
        ob[i] = (out[:, :HD] / out[:, HD:]).astype(BF).reshape(4, PT, HD)
        for d in (2, 1, 3):
            z = (zh + d) % 4
            remote(ob.at[i, z], at3.at[mine_r, rows], o_s.at[i, d], o_r.at[mine_r, i], {"seq": z * 2 + c}).start()
        at3[mine_r, rows] = ob[i, zh]

    @pl.when(active)
    def _():
        attend(0)

    enc = part[c, zh] + e1r[zh]
    for d in (1, 2, 3):
        remote(e2s.at[d], e2r.at[d], e_s.at[d], e_r.at[d], at_sib).wait_recv()
        enc = enc + e2r[d].astype(F32)
    loads[2].wait()
    loads[3].wait()
    average = jnp.mean(enc, axis=1, keepdims=True)
    centred = enc - average
    variance = jnp.mean(centred * centred, axis=1, keepdims=True)
    normed = (
        centred * lax.rsqrt(variance + layer_eps) * gain[...].reshape(1, E) + bias[...].reshape(1, E)
    ).astype(BF)
    for e in range(4):
        tn[e, zh] = normed[:, e * EC : (e + 1) * EC]
    for d in (2, 1, 3):
        to = (zh + d) % 4
        go(remote(tn.at[:, zh], tn.at[:, zh], t_s.at[d], t_r.at[4 - d], {"seq": to * 2 + c}))

    @pl.when(active)
    def _():
        attend(1)
        attend(2)

    for d in (1, 2, 3):
        fr = (zh + d) % 4
        remote(tn.at[:, fr], tn.at[:, fr], t_s.at[d], t_r.at[d], at_sib).wait_recv()
    for d in (4, 3, 5, 2, 6, 1, 7):
        go(remote(tn.at[(y + d) % 4], tb.at[y, c], ty_s.at[d], ty_r.at[8 - d], at_y(d)))
    tb[y, c] = tn[chunk]

    def gather_start(at, ss, rs):
        for n, d in enumerate((2, 6, 1, 7)):
            go(remote(at(y), at(y), ss(n), rs(8 - d), at_y(d)))

    def gather_took(at, rs, d):
        fr = (y + d) % 8
        remote(at(fr), at(fr), rs(d), rs(d), at_y(d)).wait_recv()

    def gather_relay(at, ss, rs):
        gather_took(at, rs, 6)
        lo = (y + 6) % 8
        gather_took(at, rs, 2)
        hi = (y + 2) % 8
        far = (y + 6 + 4 * odd) % 8
        go(remote(at(far), at(far), ss(6), rs(4), at_y(2 + 4 * odd)))
        go(remote(at(lo), at(lo), ss(4), rs(5), at_y(1)))
        go(remote(at(hi), at(hi), ss(5), rs(3), at_y(7)))

    loads[5].wait()

    for i in range(PH):
        rows = slice(i * PT, (i + 1) * PT)
        for r, worker in enumerate(workers):

            @pl.when(worker != zh)
            def _(r=r, rows=rows, i=i):
                remote(at3.at[r, rows], at3.at[r, rows], o_r.at[r, i], o_r.at[r, i], at_sib).wait_recv()

        attn[rows, :] = jnp.concatenate([at3[r, rows] for r in range(NH)], axis=1)
        partial = lax.dot_general(
            attn[rows, :], w[...], (((1,), (1,)), ((), ())), preferred_element_type=F32
        )
        for t in range(2):
            for e in range(4):
                pp[i, t * 4 + e] = partial[t * SUB : (t + 1) * SUB, e * EC : (e + 1) * EC]
        sf[i] = pp[i, (y + 4) % 8].astype(BF)
        go(remote(sf.at[i], rf.at[i], p_s.at[i, 0], p_r.at[i, 0], at_y(2 + 4 * odd)))
        s1[i, 0, 1] = pp[i, (y + 3) % 8].astype(BF)
        s1[i, 0, 0] = pp[i, (y + 1) % 8].astype(BF)
        go(remote(s1.at[i, 0], r1.at[i, 0], p_s.at[i, 1], p_r.at[i, 1], at_y(1)))
        s1[i, 1, 1] = pp[i, (y + 5) % 8].astype(BF)
        s1[i, 1, 0] = pp[i, (y + 7) % 8].astype(BF)
        go(remote(s1.at[i, 1], r1.at[i, 1], p_s.at[i, 2], p_r.at[i, 2], at_y(7)))
    for d in range(1, 8):
        fr = (y + d) % 8
        remote(tb.at[fr, c], tb.at[fr, c], ty_s.at[d], ty_r.at[d], at_y(d)).wait_recv()
    to_core = remote(tb.at[:, c], tb.at[:, c], tc_s.at[0], tc_r.at[0], at_sib)
    go(to_core)
    for i in range(PH):
        remote(sf.at[i], rf.at[i], p_s.at[i, 0], p_r.at[i, 0], at_y(1)).wait_recv()
        remote(s1.at[i, 0], r1.at[i, 0], p_s.at[i, 1], p_r.at[i, 1], at_y(1)).wait_recv()
        remote(s1.at[i, 1], r1.at[i, 1], p_s.at[i, 2], p_r.at[i, 2], at_y(7)).wait_recv()
        far = rf[i].astype(F32)
        upper = pp[i, (y + 2) % 8] + r1[i, 0, 1].astype(F32)
        lower = pp[i, (y + 6) % 8] + r1[i, 1, 1].astype(F32)
        s2[i, 0] = jnp.where(odd == 0, upper + far, upper).astype(BF)
        go(remote(s2.at[i, 0], r2.at[i, 0], p_s.at[i, 3], p_r.at[i, 3], at_y(2)))
        s2[i, 1] = jnp.where(odd == 1, lower + far, lower).astype(BF)
        go(remote(s2.at[i, 1], r2.at[i, 1], p_s.at[i, 4], p_r.at[i, 4], at_y(6)))

    loads[4].wait()
    picks = idx[...]
    rest = picks % 128
    spot = picks // 128 * 128 + rest // 16 % 2 * 64 + rest // 32 * 16 + rest % 16
    hot = (lax.broadcasted_iota(jnp.int32, (1024, TOK), 0) == spot).astype(F32).astype(BF)
    remote(tb.at[:, o], tb.at[:, o], tc_s.at[0], tc_r.at[0], at_sib).wait_recv()
    aligned[...] = lax.dot_general(
        hot, tb[...].reshape(1024, EC), (((0,), (0,)), ((), ())), preferred_element_type=F32
    )

    lane = lax.broadcasted_iota(jnp.int32, (128, 128), 1)
    sub = lax.broadcasted_iota(jnp.int32, (128, 128), 0)

    def tall(column):
        return jnp.concatenate([column, jnp.zeros((128 - SUB, 1), F32)], axis=0)

    def own_rows(i):
        return pl.ds(pl.multiple_of(i * PT + half * SUB, 16), SUB)

    for i in range(PH):
        remote(s2.at[i, 0], r2.at[i, 0], p_s.at[i, 3], p_r.at[i, 3], at_y(2)).wait_recv()
        remote(s2.at[i, 1], r2.at[i, 1], p_s.at[i, 4], p_r.at[i, 4], at_y(6)).wait_recv()
        proj = (
            pp[i, y]
            + (r1[i, 0, 0].astype(F32) + r1[i, 1, 0].astype(F32))
            + (r2[i, 0].astype(F32) + r2[i, 1].astype(F32))
        )
        pp[i, y] = proj
        al = aligned[own_rows(i), :]
        sums = [jnp.sum(v, axis=1, keepdims=True) for v in (proj * proj, proj * al, al * al)]
        packed = jnp.where(
            lane == 0, tall(sums[0]), jnp.where(lane == 1, tall(sums[1]), jnp.where(lane == 2, tall(sums[2]), 0.0))
        )
        stat[i, chunk] = packed.T[0:8, :]
        for d in (2, 1, 3):
            to = half * 4 + (chunk + d) % 4
            go(remote(stat.at[i, chunk], stat.at[i, chunk], st_s.at[i, d], st_r.at[i, 4 - d], {"head": to}))

    def grad_at(i):
        return (lambda n: pr.at[i, n]), (lambda n: a_s.at[i, n]), (lambda n: a_r.at[i, n])

    for i in range(PH):
        for d in (1, 2, 3):
            fr = (chunk + d) % 4
            remote(stat.at[i, fr], stat.at[i, fr], st_s.at[i, d], st_r.at[i, d], at_sib).wait_recv()
        total = (stat[i, 0] + stat[i, 1]) + (stat[i, 2] + stat[i, 3])
        pn = jnp.sqrt(total[0:1] + cos_eps)
        an = jnp.sqrt(total[2:3] + cos_eps)
        cos = total[1:2] / (pn * an)
        cosx[0, i] = jnp.broadcast_to(cos, (8, 128))
        factors = jnp.where(sub == 0, 1.0 / (pn * an), jnp.where(sub == 1, cos / (pn * pn), 0.0)).T
        al = aligned[own_rows(i), :]
        pr[i, y] = (-(al * factors[:SUB, 0:1] - factors[:SUB, 1:2] * pp[i, y])).astype(BF)
        gather_start(*grad_at(i))
    go(remote(cosx.at[0], cosx.at[1], c_s.at[0], c_r.at[0], at_y(4)))
    for i in range(PH):
        gather_relay(*grad_at(i))
    for i in range(PH):
        at, ss, rs = grad_at(i)
        for d in (1, 7, 3, 5, 4):
            gather_took(at, rs, d)

    def grad_columns(e):
        return jnp.concatenate([pr[i, t * 4 + e] for i in range(PH) for t in range(2)], axis=0)

    xo, xu, xd = (x + 2) % 4, (x + 1) % 4, (x + 3) % 4
    for n, xx in enumerate((xo, xu, xd, x)):
        block = lax.dot_general(grad_columns(xx), attn[...], (((0,), (0,)), ((), ())), preferred_element_type=F32)
        for zz in range(2):
            own[xx, zz] = block[zz * BLK : (zz + 1) * BLK]
        g1s[n] = own[xx, o].astype(BF)
        go(remote(g1s.at[n], g1r.at[n], g_s.at[n], g_r.at[n], at_sib))
    for n, (xx, d) in enumerate(((xo, 2), (xu, 1), (xd, 3))):
        remote(g1s.at[n], g1r.at[n], g_s.at[n], g_r.at[n], at_sib).wait_recv()
        g2s[n] = (own[xx, c] + g1r[n].astype(F32)).astype(BF)
        first_rows = slice(0, HB)
        go(remote(g2s.at[n, first_rows], g2r.at[4 - d, first_rows], x_s.at[0, d], x_r.at[0, 4 - d], {"dp": xx * 2 + zl}))
    for n, (xx, d) in enumerate(((xo, 2), (xu, 1), (xd, 3))):
        last_rows = slice(HB, BLK)
        go(remote(g2s.at[n, last_rows], g2r.at[4 - d, last_rows], x_s.at[1, d], x_r.at[1, 4 - d], {"dp": xx * 2 + zl}))
    back = jnp.dot(grad_columns(0), w[:EC], preferred_element_type=F32)
    for e in range(1, 4):
        back = back + jnp.dot(grad_columns(e), w[e * EC : (e + 1) * EC], preferred_element_type=F32)
    grad_attn[...] = back.astype(BF)
    remote(g1s.at[3], g1r.at[3], g_s.at[3], g_r.at[3], at_sib).wait_recv()
    for part_of in range(2):
        rows = slice(part_of * HB, (part_of + 1) * HB)
        mine = own[x, c, rows] + g1r[3, rows].astype(F32)
        for d in (1, 3, 2):
            remote(g2s.at[0, rows], g2r.at[d, rows], x_s.at[part_of, d], x_r.at[part_of, d], at_sib).wait_recv()
            mine = mine + g2r[d, rows].astype(F32)
        for n in range(4):
            piece = jnp.concatenate([mine[n * 24 : (n + 1) * 24], jnp.zeros((8, DA), F32)], axis=0)
            g3s[part_of * 4 + n] = piece.astype(BF)
        for n in range(4):
            tz, cc = part_of * 2 + n // 2, n % 2
            go_if(
                (tz != zh) | (zl != c) | (c != cc),
                remote(g3s.at[tz * 2 + cc], g3r.at[pos], z_s.at[tz, cc], z_r.at[pos],
                       {"dp": x * 2 + c, "seq": tz * 2 + cc}),
            )
    row = jnp.zeros((8, 384), F32)
    token = lax.broadcasted_iota(jnp.int32, (8, 384), 1)
    remote(cosx.at[0], cosx.at[1], c_s.at[0], c_r.at[0], at_y(4)).wait_recv()
    for n in range(2):
        for i in range(PH):
            start = i * PT + (half + (1 - 2 * half) * n) * SUB
            wide = jnp.concatenate([cosx[n, i], jnp.zeros((8, 256), F32)], axis=1)
            inside = (token >= start) & (token < start + SUB)
            row = jnp.where(inside, pltpu.roll(wide, start, 1), row)
    cos_out[...] = row[0:1, :TOK]

    @pl.when(zl == c)
    def _():
        g3r[pos] = g3s[zh * 2 + c]

    @pl.when(zl != c)
    def _():
        remote(g3s.at[0], g3r.at[pos], z_s.at[0, 0], z_r.at[pos], at_sib).wait_recv()

    for d in range(1, 8):
        fr = (pos + d) % 8
        remote(g3s.at[0], g3r.at[fr], z_s.at[0, 0], z_r.at[fr], at_sib).wait_recv()
    total = g3r[0].astype(F32)
    for n in range(1, 8):
        total = total + g3r[n].astype(F32)
    grad_proj[...] = total[:24]

    @pl.when(active)
    def _():
        for z in range(4):
            for buf, ss in ((kb, ks_s), (vb, vs_s)):
                remote(buf.at[z * 2 + c], buf.at[z * 2 + c], ss.at[z], ks_r.at[z], at_sib).wait_send()
        for i in range(PH):
            for d in (1, 2, 3):
                remote(ob.at[i, d], at3.at[0, :PT], o_s.at[i, d], o_r.at[0, i], at_sib).wait_send()

    for cond, copy in cond_sent:

        @pl.when(cond)
        def _(copy=copy):
            copy.wait_send()

    for copy in sent:
        copy.wait_send()


def settle(a, b, c, d, a_out, b_out, c_out, d_out, a_in, b_in, c_in, d_in, sems):
    first = [
        pltpu.make_async_copy(src, dst, sems.at[n])
        for n, (src, dst) in enumerate(((a, a_in), (b, b_in), (c, c_in), (d, d_in)))
    ]
    second = [
        pltpu.make_async_copy(src, dst, sems.at[n + 4])
        for n, (src, dst) in enumerate(((a_in, a_out), (b_in, b_out), (c_in, c_out), (d_in, d_out)))
    ]
    for copy in first:
        copy.start()
    for one, two in zip(first, second):
        one.wait()
        two.start()
    for copy in second:
        copy.wait()


def on_device(patch_in, enc_weight, enc_gain, enc_bias, interp_index, queries, key_rows, value_rows, proj_weight):
    vm = pl.BlockSpec(memory_space=pltpu.VMEM)
    hbm = pl.BlockSpec(memory_space=pltpu.HBM)
    dma = pltpu.SemaphoreType.DMA
    attn, cosine, grad_attn, grad_proj = pl.pallas_call(
        kernel,
        out_shape=(
            jax.ShapeDtypeStruct((TOK, DA), BF),
            jax.ShapeDtypeStruct((1, TOK), F32),
            jax.ShapeDtypeStruct((TOK, DA), BF),
            jax.ShapeDtypeStruct((24, DA), F32),
        ),
        in_specs=[hbm] * 9,
        out_specs=(vm,) * 4,
        scratch_shapes=[
            pltpu.VMEM((192, 128), BF),
            pltpu.VMEM((192, E), BF),
            pltpu.VMEM((E,), F32),
            pltpu.VMEM((E,), F32),
            pltpu.VMEM((1, TOK), jnp.int32),
            pltpu.VMEM((E, DA), BF),
            pltpu.VMEM((NH, TOK, HD), BF),
            pltpu.VMEM((NH, TOK, HD), BF),
            pltpu.VMEM((NH, TOK, HD), BF),
            pltpu.VMEM((PH, 4, PT, HD), BF),
            pltpu.VMEM((8, TOK, HD), BF),
            pltpu.VMEM((8, TOK, HD), BF),
            pltpu.VMEM((PH, 4, PT, HD), BF),
            pltpu.VMEM((NH, TOK, HD), BF),
            pltpu.VMEM((2, 4, 16, E), F32),
            pltpu.VMEM((4, 16, E), F32),
            pltpu.VMEM((4, 16, E), BF),
            pltpu.VMEM((4, 16, E), BF),
            pltpu.VMEM((4, 4, 16, EC), BF),
            pltpu.VMEM((8, 2, 4, 16, EC), BF),
            pltpu.VMEM((TOK, EC), F32),
            pltpu.VMEM((PH, 8, SUB, EC), F32),
            pltpu.VMEM((PH, 2, 2, SUB, EC), BF),
            pltpu.VMEM((PH, 2, 2, SUB, EC), BF),
            pltpu.VMEM((PH, SUB, EC), BF),
            pltpu.VMEM((PH, SUB, EC), BF),
            pltpu.VMEM((PH, 2, SUB, EC), BF),
            pltpu.VMEM((PH, 2, SUB, EC), BF),
            pltpu.VMEM((PH, 8, SUB, EC), BF),
            pltpu.VMEM((PH, 4, 8, 128), F32),
            pltpu.VMEM((2, PH, 8, 128), F32),
            pltpu.VMEM((4, 2, BLK, DA), F32),
            pltpu.VMEM((4, BLK, DA), BF),
            pltpu.VMEM((4, BLK, DA), BF),
            pltpu.VMEM((3, BLK, DA), BF),
            pltpu.VMEM((4, BLK, DA), BF),
            pltpu.VMEM((8, 32, DA), BF),
            pltpu.VMEM((8, 32, DA), BF),
            dma((6,)),
            dma((3, NH)),
            dma((NH,)),
            dma((4,)),
            dma((4,)),
            dma((4,)),
            dma((NH,)),
            dma((4,)),
            dma((4,)),
            dma((4,)),
            dma((PH, NH)),
            dma((PH, 4)),
            dma((PH, 4)),
            dma((NH, PH)),
            dma((4,)),
            dma((4,)),
            dma((4,)),
            dma((4,)),
            dma((8,)),
            dma((8,)),
            dma((8,)),
            dma((8,)),
            dma((PH, 5)),
            dma((PH, 5)),
            dma((PH, 4)),
            dma((PH, 4)),
            dma((1,)),
            dma((1,)),
            dma((PH, 8)),
            dma((PH, 8)),
            dma((4,)),
            dma((4,)),
            dma((2, 4)),
            dma((2, 4)),
            dma((4, 2)),
            dma((8,)),
        ],
        compiler_params=pltpu.CompilerParams(
            collective_id=0, has_side_effects=True, vmem_limit_bytes=56 * 2**20
        ),
        name="whole",
    )(
        patch_in[0].T,
        enc_weight,
        enc_gain,
        enc_bias,
        interp_index,
        queries[0],
        key_rows[0],
        value_rows[0],
        proj_weight,
    )
    results = (attn, cosine, grad_attn, grad_proj)
    attn, cosine, grad_attn, grad_proj = pl.pallas_call(
        settle,
        out_shape=tuple(jax.ShapeDtypeStruct(a.shape, a.dtype) for a in results),
        in_specs=[hbm] * 4,
        out_specs=(hbm,) * 4,
        scratch_shapes=[pltpu.VMEM(a.shape, a.dtype) for a in results] + [dma((8,))],
        compiler_params=pltpu.CompilerParams(vmem_limit_bytes=60 * 2**20),
        name="settle",
    )(*results)
    return attn[None], cosine, grad_attn[None], grad_proj


def solution(mesh):
    placed = (
        P("dp", "head", "seq"),
        P("seq", None),
        P(),
        P(),
        P("dp", "seq"),
        P("dp", "seq", "head"),
        P("dp", "seq", "head"),
        P("dp", "seq", "head"),
        P(None, "head"),
    )
    return jax.shard_map(
        on_device,
        mesh=mesh,
        in_specs=placed,
        out_specs=(
            P("dp", "seq", "head"),
            P("dp", "seq"),
            P("dp", "seq", "head"),
            P(("dp", "seq"), "head"),
        ),
        check_vma=False,
    )
```

```python
import jax
import jax.numpy as jnp
from jax import lax
from jax.experimental import pallas as pl
from jax.experimental.pallas import tpu as pltpu
from jax.sharding import PartitionSpec as P

MESH = pl.DeviceIdType.MESH
BF = jnp.bfloat16
F32 = jnp.float32

E = 1536
HD = 128
NH = 3
DA = NH * HD
TOK = 288
SUB = 48
EC = 384
PH = 3
PT = 2 * SUB
HB = 96
BLK = 192

layer_eps = 1e-06
cos_eps = 1e-06
EXP_SCALE = HD**-0.5 * 1.4426950408889634


def remote(src, dst, send, recv, where):
    return pltpu.make_async_remote_copy(
        src_ref=src, dst_ref=dst, send_sem=send, recv_sem=recv, device_id=where, device_id_type=MESH
    )


def kernel(
    patch_h, enc_h, gain_h, bias_h, idx_h, q_h, k_h, v_h, w_h,
    attn, cos_out, grad_attn, grad_proj,
    patch, enc_w, gain, bias, idx, w, q3, k3, v3,
    qb, kb, vb, ob, at3, part, e1r, e2s, e2r, tn, tb, aligned,
    pp, s1, r1, sf, rf, s2, r2, pr, stat, cosx,
    own, g1s, g1r, g2s, g2r, g3s, g3r,
    l_s, l3_s, k_s, k_r, ks_s, ks_r, v_s, v_r, vs_s, vs_r, q_s, q_r, o_s, o_r, e_s, e_r, t_s, t_r, ty_s, ty_r, tc_s, tc_r,
    p_s, p_r, st_s, st_r, c_s, c_r, a_s, a_r, g_s, g_r, x_s, x_r, z_s, z_r,
):
    dp, seq, y = lax.axis_index("dp"), lax.axis_index("seq"), lax.axis_index("head")
    x, zl, zh, c = dp // 2, dp % 2, seq // 2, seq % 2
    o = 1 - c
    odd = y % 2
    half, chunk = y // 4, y % 4
    pos = zh * 2 + zl
    at_sib = {"seq": zh * 2 + o}
    sent = []

    def at_y(d):
        return {"head": (y + d) % 8}

    def go(copy):
        copy.start()
        sent.append(copy)

    loads = [
        pltpu.make_async_copy(src, dst, l_s.at[n])
        for n, (src, dst) in enumerate(
            ((patch_h, patch), (enc_h, enc_w), (gain_h, gain), (bias_h, bias), (idx_h, idx), (w_h, w))
        )
    ]
    qkv_loads = [
        [
            pltpu.make_async_copy(src.at[:, h * HD : (h + 1) * HD], dst.at[h], l3_s.at[n, h])
            for h in range(NH)
        ]
        for n, (src, dst) in enumerate(((k_h, k3), (v_h, v3), (q_h, q3)))
    ]
    for copy in (*loads[:2], *qkv_loads[0], *qkv_loads[1], *qkv_loads[2], *loads[2:]):
        copy.start()

    barrier = pltpu.get_barrier_semaphore()
    peers = [at_y(d) for d in range(1, 8)]
    peers += [{"dp": (x + d) % 4 * 2 + zl} for d in (1, 2, 3)]
    peers += [at_sib]
    for d in range(1, 8):
        to = (pos + d) % 8
        for cc in range(2):
            peers.append({"dp": x * 2 + to % 2, "seq": to // 2 * 2 + cc})
    for peer in peers:
        pl.semaphore_signal(barrier, inc=1, device_id=peer, device_id_type=MESH)
    loads[0].wait()
    loads[1].wait()
    share = lax.dot_general(
        patch[...], enc_w[...], (((0,), (0,)), ((), ())), preferred_element_type=F32
    )
    for z in range(4):
        for cc in range(2):
            part[cc, z] = share[(2 * z + cc) * 16 : (2 * z + cc + 1) * 16]
    for group in qkv_loads:
        for copy in group:
            copy.wait()
    pl.semaphore_wait(barrier, len(peers))

    first = 2 * zl + 1
    mine_r = (zh + 4 - first) % 4
    active = mine_r < NH
    workers = [(first + r) % 4 for r in range(NH)]
    cond_sent = []

    def go_if(cond, copy):
        cond_sent.append((cond, copy))

        @pl.when(cond)
        def _():
            copy.start()

    def scatter(src, buf, ss, rs):
        for r, worker in enumerate(workers):
            go_if(worker != zh, remote(src.at[r], buf.at[seq], ss.at[r], rs.at[zh], {"seq": worker * 2 + c}))

    def to_sib(buf, ss, rs, z):
        copy = remote(buf.at[z * 2 + c], buf.at[z * 2 + c], ss.at[z], rs.at[z], at_sib)
        copy.start()
        return copy

    def keep(src, buf, ss, rs):
        @pl.when(active)
        def _():
            buf[seq] = src[mine_r]
            to_sib(buf, ss, rs, zh)

    def pass_on(buf, rs, ss2, rs2):
        @pl.when(active)
        def _():
            for d in (1, 3, 2):
                z = (zh + d) % 4
                remote(buf.at[z * 2 + c], buf.at[z * 2 + c], rs.at[z], rs.at[z], at_sib).wait_recv()
                to_sib(buf, ss2, rs2, z)

    scatter(k3, kb, k_s, k_r)
    scatter(v3, vb, v_s, v_r)
    for i in range(PH):
        rows = slice(i * PT, (i + 1) * PT)
        for r, worker in enumerate(workers):
            go_if(
                worker != zh,
                remote(q3.at[r, rows], qb.at[i, zh], q_s.at[i, r], q_r.at[i, zh], {"seq": worker * 2 + c}),
            )
    keep(k3, kb, ks_s, ks_r)
    keep(v3, vb, vs_s, vs_r)
    e1 = remote(part.at[o], e1r, e_s.at[0], e_r.at[0], at_sib)
    go(e1)
    e1.wait_recv()
    pass_on(kb, k_r, ks_s, ks_r)
    for d in (2, 1, 3):
        to = (zh + d) % 4
        e2s[d] = (part[c, to] + e1r[to]).astype(BF)
        go(remote(e2s.at[d], e2r.at[4 - d], e_s.at[d], e_r.at[4 - d], {"seq": to * 2 + c}))
    pass_on(vb, v_r, vs_s, vs_r)

    @pl.when(active)
    def _():
        for buf, rs in ((kb, ks_r), (vb, vs_r)):
            for z in range(4):
                remote(buf.at[z * 2 + o], buf.at[z * 2 + o], rs.at[z], rs.at[z], at_sib).wait_recv()

    def attend(i):
        rows = slice(i * PT, (i + 1) * PT)
        qb[i, zh] = q3[mine_r, rows]
        for d in (1, 3, 2):
            z = (zh + d) % 4
            remote(qb.at[i, z], qb.at[i, z], q_r.at[i, z], q_r.at[i, z], at_sib).wait_recv()
        scores = lax.dot_general(
            qb[i].reshape(4 * PT, HD), kb[...].reshape(8 * TOK, HD), (((1,), (1,)), ((), ())),
            preferred_element_type=F32,
        )
        top = jnp.max(scores, axis=1, keepdims=True)
        expo = jnp.exp2((scores - top) * EXP_SCALE).astype(BF)
        wide = jnp.concatenate([vb[...].reshape(8 * TOK, HD), jnp.ones((8 * TOK, HD), BF)], axis=1)
        out = jnp.dot(expo, wide, preferred_element_type=F32)
        ob[i] = (out[:, :HD] / out[:, HD:]).astype(BF).reshape(4, PT, HD)
        for d in (2, 1, 3):
            z = (zh + d) % 4
            remote(ob.at[i, z], at3.at[mine_r, rows], o_s.at[i, d], o_r.at[mine_r, i], {"seq": z * 2 + c}).start()
        at3[mine_r, rows] = ob[i, zh]

    @pl.when(active)
    def _():
        attend(0)

    enc = part[c, zh] + e1r[zh]
    for d in (1, 2, 3):
        remote(e2s.at[d], e2r.at[d], e_s.at[d], e_r.at[d], at_sib).wait_recv()
        enc = enc + e2r[d].astype(F32)
    loads[2].wait()
    loads[3].wait()
    average = jnp.mean(enc, axis=1, keepdims=True)
    centred = enc - average
    variance = jnp.mean(centred * centred, axis=1, keepdims=True)
    normed = (
        centred * lax.rsqrt(variance + layer_eps) * gain[...].reshape(1, E) + bias[...].reshape(1, E)
    ).astype(BF)
    for e in range(4):
        tn[e, zh] = normed[:, e * EC : (e + 1) * EC]
    for d in (2, 1, 3):
        to = (zh + d) % 4
        go(remote(tn.at[:, zh], tn.at[:, zh], t_s.at[d], t_r.at[4 - d], {"seq": to * 2 + c}))

    @pl.when(active)
    def _():
        attend(1)
        attend(2)

    def gather_start(at, ss, rs):
        for n, d in enumerate((2, 6, 1, 7)):
            go(remote(at(y), at(y), ss(n), rs(8 - d), at_y(d)))

    def gather_took(at, rs, d):
        fr = (y + d) % 8
        remote(at(fr), at(fr), rs(d), rs(d), at_y(d)).wait_recv()

    def gather_relay(at, ss, rs):
        gather_took(at, rs, 6)
        lo = (y + 6) % 8
        gather_took(at, rs, 2)
        hi = (y + 2) % 8
        far = (y + 6 + 4 * odd) % 8
        go(remote(at(far), at(far), ss(6), rs(4), at_y(2 + 4 * odd)))
        go(remote(at(lo), at(lo), ss(4), rs(5), at_y(1)))
        go(remote(at(hi), at(hi), ss(5), rs(3), at_y(7)))

    loads[5].wait()

    for i in range(PH):
        rows = slice(i * PT, (i + 1) * PT)
        for r, worker in enumerate(workers):

            @pl.when(worker != zh)
            def _(r=r, rows=rows, i=i):
                remote(at3.at[r, rows], at3.at[r, rows], o_r.at[r, i], o_r.at[r, i], at_sib).wait_recv()

        attn[rows, :] = jnp.concatenate([at3[r, rows] for r in range(NH)], axis=1)
        partial = lax.dot_general(
            attn[rows, :], w[...], (((1,), (1,)), ((), ())), preferred_element_type=F32
        )
        for t in range(2):
            for e in range(4):
                pp[i, t * 4 + e] = partial[t * SUB : (t + 1) * SUB, e * EC : (e + 1) * EC]
        sf[i] = pp[i, (y + 4) % 8].astype(BF)
        go(remote(sf.at[i], rf.at[i], p_s.at[i, 0], p_r.at[i, 0], at_y(2 + 4 * odd)))
        s1[i, 0, 1] = pp[i, (y + 3) % 8].astype(BF)
        s1[i, 0, 0] = pp[i, (y + 1) % 8].astype(BF)
        go(remote(s1.at[i, 0], r1.at[i, 0], p_s.at[i, 1], p_r.at[i, 1], at_y(1)))
        s1[i, 1, 1] = pp[i, (y + 5) % 8].astype(BF)
        s1[i, 1, 0] = pp[i, (y + 7) % 8].astype(BF)
        go(remote(s1.at[i, 1], r1.at[i, 1], p_s.at[i, 2], p_r.at[i, 2], at_y(7)))
    for d in (1, 2, 3):
        fr = (zh + d) % 4
        remote(tn.at[:, fr], tn.at[:, fr], t_s.at[d], t_r.at[d], at_sib).wait_recv()
    for d in (4, 3, 5, 2, 6, 1, 7):
        go(remote(tn.at[(y + d) % 4], tb.at[y, c], ty_s.at[d], ty_r.at[8 - d], at_y(d)))
    tb[y, c] = tn[chunk]

    for i in range(PH):
        remote(sf.at[i], rf.at[i], p_s.at[i, 0], p_r.at[i, 0], at_y(1)).wait_recv()
        remote(s1.at[i, 0], r1.at[i, 0], p_s.at[i, 1], p_r.at[i, 1], at_y(1)).wait_recv()
        remote(s1.at[i, 1], r1.at[i, 1], p_s.at[i, 2], p_r.at[i, 2], at_y(7)).wait_recv()
        far = rf[i].astype(F32)
        upper = pp[i, (y + 2) % 8] + r1[i, 0, 1].astype(F32)
        lower = pp[i, (y + 6) % 8] + r1[i, 1, 1].astype(F32)
        s2[i, 0] = jnp.where(odd == 0, upper + far, upper).astype(BF)
        go(remote(s2.at[i, 0], r2.at[i, 0], p_s.at[i, 3], p_r.at[i, 3], at_y(2)))
        s2[i, 1] = jnp.where(odd == 1, lower + far, lower).astype(BF)
        go(remote(s2.at[i, 1], r2.at[i, 1], p_s.at[i, 4], p_r.at[i, 4], at_y(6)))

    for d in range(1, 8):
        fr = (y + d) % 8
        remote(tb.at[fr, c], tb.at[fr, c], ty_s.at[d], ty_r.at[d], at_y(d)).wait_recv()
    to_core = remote(tb.at[:, c], tb.at[:, c], tc_s.at[0], tc_r.at[0], at_sib)
    go(to_core)
    loads[4].wait()
    picks = idx[...]
    rest = picks % 128
    spot = picks // 128 * 128 + rest // 16 % 2 * 64 + rest // 32 * 16 + rest % 16
    hot = (lax.broadcasted_iota(jnp.int32, (1024, TOK), 0) == spot).astype(F32).astype(BF)
    remote(tb.at[:, o], tb.at[:, o], tc_s.at[0], tc_r.at[0], at_sib).wait_recv()
    aligned[...] = lax.dot_general(
        hot, tb[...].reshape(1024, EC), (((0,), (0,)), ((), ())), preferred_element_type=F32
    )

    lane = lax.broadcasted_iota(jnp.int32, (128, 128), 1)
    sub = lax.broadcasted_iota(jnp.int32, (128, 128), 0)

    def tall(column):
        return jnp.concatenate([column, jnp.zeros((128 - SUB, 1), F32)], axis=0)

    def own_rows(i):
        return pl.ds(pl.multiple_of(i * PT + half * SUB, 16), SUB)

    for i in range(PH):
        remote(s2.at[i, 0], r2.at[i, 0], p_s.at[i, 3], p_r.at[i, 3], at_y(2)).wait_recv()
        remote(s2.at[i, 1], r2.at[i, 1], p_s.at[i, 4], p_r.at[i, 4], at_y(6)).wait_recv()
        proj = (
            pp[i, y]
            + (r1[i, 0, 0].astype(F32) + r1[i, 1, 0].astype(F32))
            + (r2[i, 0].astype(F32) + r2[i, 1].astype(F32))
        )
        pp[i, y] = proj
        al = aligned[own_rows(i), :]
        sums = [jnp.sum(v, axis=1, keepdims=True) for v in (proj * proj, proj * al, al * al)]
        packed = jnp.where(
            lane == 0, tall(sums[0]), jnp.where(lane == 1, tall(sums[1]), jnp.where(lane == 2, tall(sums[2]), 0.0))
        )
        stat[i, chunk] = packed.T[0:8, :]
        for d in (2, 1, 3):
            to = half * 4 + (chunk + d) % 4
            go(remote(stat.at[i, chunk], stat.at[i, chunk], st_s.at[i, d], st_r.at[i, 4 - d], {"head": to}))

    def grad_at(i):
        return (lambda n: pr.at[i, n]), (lambda n: a_s.at[i, n]), (lambda n: a_r.at[i, n])

    for i in range(PH):
        for d in (1, 2, 3):
            fr = (chunk + d) % 4
            remote(stat.at[i, fr], stat.at[i, fr], st_s.at[i, d], st_r.at[i, d], at_sib).wait_recv()
        total = (stat[i, 0] + stat[i, 1]) + (stat[i, 2] + stat[i, 3])
        pn = jnp.sqrt(total[0:1] + cos_eps)
        an = jnp.sqrt(total[2:3] + cos_eps)
        cos = total[1:2] / (pn * an)
        cosx[0, i] = jnp.broadcast_to(cos, (8, 128))
        factors = jnp.where(sub == 0, 1.0 / (pn * an), jnp.where(sub == 1, cos / (pn * pn), 0.0)).T
        al = aligned[own_rows(i), :]
        pr[i, y] = (-(al * factors[:SUB, 0:1] - factors[:SUB, 1:2] * pp[i, y])).astype(BF)
        gather_start(*grad_at(i))
    go(remote(cosx.at[0], cosx.at[1], c_s.at[0], c_r.at[0], at_y(4)))
    for i in range(PH):
        gather_relay(*grad_at(i))
    for i in range(PH):
        at, ss, rs = grad_at(i)
        for d in (1, 7, 3, 5, 4):
            gather_took(at, rs, d)

    def grad_columns(e):
        return jnp.concatenate([pr[i, t * 4 + e] for i in range(PH) for t in range(2)], axis=0)

    xo, xu, xd = (x + 2) % 4, (x + 1) % 4, (x + 3) % 4
    for n, xx in enumerate((xo, xu, xd, x)):
        block = lax.dot_general(grad_columns(xx), attn[...], (((0,), (0,)), ((), ())), preferred_element_type=F32)
        for zz in range(2):
            own[xx, zz] = block[zz * BLK : (zz + 1) * BLK]
        g1s[n] = own[xx, o].astype(BF)
        go(remote(g1s.at[n], g1r.at[n], g_s.at[n], g_r.at[n], at_sib))
    for n, (xx, d) in enumerate(((xo, 2), (xu, 1), (xd, 3))):
        remote(g1s.at[n], g1r.at[n], g_s.at[n], g_r.at[n], at_sib).wait_recv()
        g2s[n] = (own[xx, c] + g1r[n].astype(F32)).astype(BF)
        first_rows = slice(0, HB)
        go(remote(g2s.at[n, first_rows], g2r.at[4 - d, first_rows], x_s.at[0, d], x_r.at[0, 4 - d], {"dp": xx * 2 + zl}))
    for n, (xx, d) in enumerate(((xo, 2), (xu, 1), (xd, 3))):
        last_rows = slice(HB, BLK)
        go(remote(g2s.at[n, last_rows], g2r.at[4 - d, last_rows], x_s.at[1, d], x_r.at[1, 4 - d], {"dp": xx * 2 + zl}))
    back = jnp.dot(grad_columns(0), w[:EC], preferred_element_type=F32)
    for e in range(1, 4):
        back = back + jnp.dot(grad_columns(e), w[e * EC : (e + 1) * EC], preferred_element_type=F32)
    grad_attn[...] = back.astype(BF)
    remote(g1s.at[3], g1r.at[3], g_s.at[3], g_r.at[3], at_sib).wait_recv()
    for part_of in range(2):
        rows = slice(part_of * HB, (part_of + 1) * HB)
        mine = own[x, c, rows] + g1r[3, rows].astype(F32)
        for d in (1, 3, 2):
            remote(g2s.at[0, rows], g2r.at[d, rows], x_s.at[part_of, d], x_r.at[part_of, d], at_sib).wait_recv()
            mine = mine + g2r[d, rows].astype(F32)
        for n in range(4):
            piece = jnp.concatenate([mine[n * 24 : (n + 1) * 24], jnp.zeros((8, DA), F32)], axis=0)
            g3s[part_of * 4 + n] = piece.astype(BF)
        for n in range(4):
            tz, cc = part_of * 2 + n // 2, n % 2
            go_if(
                (tz != zh) | (zl != c) | (c != cc),
                remote(g3s.at[tz * 2 + cc], g3r.at[pos], z_s.at[tz, cc], z_r.at[pos],
                       {"dp": x * 2 + c, "seq": tz * 2 + cc}),
            )
    row = jnp.zeros((8, 384), F32)
    token = lax.broadcasted_iota(jnp.int32, (8, 384), 1)
    remote(cosx.at[0], cosx.at[1], c_s.at[0], c_r.at[0], at_y(4)).wait_recv()
    for n in range(2):
        for i in range(PH):
            start = i * PT + (half + (1 - 2 * half) * n) * SUB
            wide = jnp.concatenate([cosx[n, i], jnp.zeros((8, 256), F32)], axis=1)
            inside = (token >= start) & (token < start + SUB)
            row = jnp.where(inside, pltpu.roll(wide, start, 1), row)
    cos_out[...] = row[0:1, :TOK]

    @pl.when(zl == c)
    def _():
        g3r[pos] = g3s[zh * 2 + c]

    @pl.when(zl != c)
    def _():
        remote(g3s.at[0], g3r.at[pos], z_s.at[0, 0], z_r.at[pos], at_sib).wait_recv()

    for d in range(1, 8):
        fr = (pos + d) % 8
        remote(g3s.at[0], g3r.at[fr], z_s.at[0, 0], z_r.at[fr], at_sib).wait_recv()
    total = g3r[0].astype(F32)
    for n in range(1, 8):
        total = total + g3r[n].astype(F32)
    grad_proj[...] = total[:24]

    @pl.when(active)
    def _():
        for z in range(4):
            for buf, ss in ((kb, ks_s), (vb, vs_s)):
                remote(buf.at[z * 2 + c], buf.at[z * 2 + c], ss.at[z], ks_r.at[z], at_sib).wait_send()
        for i in range(PH):
            for d in (1, 2, 3):
                remote(ob.at[i, d], at3.at[0, :PT], o_s.at[i, d], o_r.at[0, i], at_sib).wait_send()

    for cond, copy in cond_sent:

        @pl.when(cond)
        def _(copy=copy):
            copy.wait_send()

    for copy in sent:
        copy.wait_send()


def settle(a, b, c, d, a_out, b_out, c_out, d_out, a_in, b_in, c_in, d_in, sems):
    first = [
        pltpu.make_async_copy(src, dst, sems.at[n])
        for n, (src, dst) in enumerate(((a, a_in), (b, b_in), (c, c_in), (d, d_in)))
    ]
    second = [
        pltpu.make_async_copy(src, dst, sems.at[n + 4])
        for n, (src, dst) in enumerate(((a_in, a_out), (b_in, b_out), (c_in, c_out), (d_in, d_out)))
    ]
    for copy in first:
        copy.start()
    for one, two in zip(first, second):
        one.wait()
        two.start()
    for copy in second:
        copy.wait()


def on_device(patch_in, enc_weight, enc_gain, enc_bias, interp_index, queries, key_rows, value_rows, proj_weight):
    vm = pl.BlockSpec(memory_space=pltpu.VMEM)
    hbm = pl.BlockSpec(memory_space=pltpu.HBM)
    dma = pltpu.SemaphoreType.DMA
    attn, cosine, grad_attn, grad_proj = pl.pallas_call(
        kernel,
        out_shape=(
            jax.ShapeDtypeStruct((TOK, DA), BF),
            jax.ShapeDtypeStruct((1, TOK), F32),
            jax.ShapeDtypeStruct((TOK, DA), BF),
            jax.ShapeDtypeStruct((24, DA), F32),
        ),
        in_specs=[hbm] * 9,
        out_specs=(vm,) * 4,
        scratch_shapes=[
            pltpu.VMEM((192, 128), BF),
            pltpu.VMEM((192, E), BF),
            pltpu.VMEM((E,), F32),
            pltpu.VMEM((E,), F32),
            pltpu.VMEM((1, TOK), jnp.int32),
            pltpu.VMEM((E, DA), BF),
            pltpu.VMEM((NH, TOK, HD), BF),
            pltpu.VMEM((NH, TOK, HD), BF),
            pltpu.VMEM((NH, TOK, HD), BF),
            pltpu.VMEM((PH, 4, PT, HD), BF),
            pltpu.VMEM((8, TOK, HD), BF),
            pltpu.VMEM((8, TOK, HD), BF),
            pltpu.VMEM((PH, 4, PT, HD), BF),
            pltpu.VMEM((NH, TOK, HD), BF),
            pltpu.VMEM((2, 4, 16, E), F32),
            pltpu.VMEM((4, 16, E), F32),
            pltpu.VMEM((4, 16, E), BF),
            pltpu.VMEM((4, 16, E), BF),
            pltpu.VMEM((4, 4, 16, EC), BF),
            pltpu.VMEM((8, 2, 4, 16, EC), BF),
            pltpu.VMEM((TOK, EC), F32),
            pltpu.VMEM((PH, 8, SUB, EC), F32),
            pltpu.VMEM((PH, 2, 2, SUB, EC), BF),
            pltpu.VMEM((PH, 2, 2, SUB, EC), BF),
            pltpu.VMEM((PH, SUB, EC), BF),
            pltpu.VMEM((PH, SUB, EC), BF),
            pltpu.VMEM((PH, 2, SUB, EC), BF),
            pltpu.VMEM((PH, 2, SUB, EC), BF),
            pltpu.VMEM((PH, 8, SUB, EC), BF),
            pltpu.VMEM((PH, 4, 8, 128), F32),
            pltpu.VMEM((2, PH, 8, 128), F32),
            pltpu.VMEM((4, 2, BLK, DA), F32),
            pltpu.VMEM((4, BLK, DA), BF),
            pltpu.VMEM((4, BLK, DA), BF),
            pltpu.VMEM((3, BLK, DA), BF),
            pltpu.VMEM((4, BLK, DA), BF),
            pltpu.VMEM((8, 32, DA), BF),
            pltpu.VMEM((8, 32, DA), BF),
            dma((6,)),
            dma((3, NH)),
            dma((NH,)),
            dma((4,)),
            dma((4,)),
            dma((4,)),
            dma((NH,)),
            dma((4,)),
            dma((4,)),
            dma((4,)),
            dma((PH, NH)),
            dma((PH, 4)),
            dma((PH, 4)),
            dma((NH, PH)),
            dma((4,)),
            dma((4,)),
            dma((4,)),
            dma((4,)),
            dma((8,)),
            dma((8,)),
            dma((8,)),
            dma((8,)),
            dma((PH, 5)),
            dma((PH, 5)),
            dma((PH, 4)),
            dma((PH, 4)),
            dma((1,)),
            dma((1,)),
            dma((PH, 8)),
            dma((PH, 8)),
            dma((4,)),
            dma((4,)),
            dma((2, 4)),
            dma((2, 4)),
            dma((4, 2)),
            dma((8,)),
        ],
        compiler_params=pltpu.CompilerParams(
            collective_id=0, has_side_effects=True, vmem_limit_bytes=56 * 2**20
        ),
        name="whole",
    )(
        patch_in[0].T,
        enc_weight,
        enc_gain,
        enc_bias,
        interp_index,
        queries[0],
        key_rows[0],
        value_rows[0],
        proj_weight,
    )
    results = (attn, cosine, grad_attn, grad_proj)
    attn, cosine, grad_attn, grad_proj = pl.pallas_call(
        settle,
        out_shape=tuple(jax.ShapeDtypeStruct(a.shape, a.dtype) for a in results),
        in_specs=[hbm] * 4,
        out_specs=(hbm,) * 4,
        scratch_shapes=[pltpu.VMEM(a.shape, a.dtype) for a in results] + [dma((8,))],
        compiler_params=pltpu.CompilerParams(vmem_limit_bytes=60 * 2**20),
        name="settle",
    )(*results)
    return attn[None], cosine, grad_attn[None], grad_proj


def solution(mesh):
    placed = (
        P("dp", "head", "seq"),
        P("seq", None),
        P(),
        P(),
        P("dp", "seq"),
        P("dp", "seq", "head"),
        P("dp", "seq", "head"),
        P("dp", "seq", "head"),
        P(None, "head"),
    )
    return jax.shard_map(
        on_device,
        mesh=mesh,
        in_specs=placed,
        out_specs=(
            P("dp", "seq", "head"),
            P("dp", "seq"),
            P("dp", "seq", "head"),
            P(("dp", "seq"), "head"),
        ),
        check_vma=False,
    )
```

```python
import jax
import jax.numpy as jnp
from jax import lax
from jax.experimental import pallas as pl
from jax.experimental.pallas import tpu as pltpu
from jax.sharding import PartitionSpec as P

MESH = pl.DeviceIdType.MESH
BF = jnp.bfloat16
F32 = jnp.float32

E = 1536
HD = 128
NH = 3
DA = NH * HD
TOK = 288
SUB = 48
EC = 384
PH = 3
PT = 2 * SUB
HB = 96
BLK = 192

layer_eps = 1e-06
cos_eps = 1e-06
EXP_SCALE = HD**-0.5 * 1.4426950408889634


def remote(src, dst, send, recv, where):
    return pltpu.make_async_remote_copy(
        src_ref=src, dst_ref=dst, send_sem=send, recv_sem=recv, device_id=where, device_id_type=MESH
    )


def kernel(
    patch_h, enc_h, gain_h, bias_h, idx_h, q_h, k_h, v_h, w_h,
    attn, cos_out, grad_attn, grad_proj,
    patch, enc_w, gain, bias, idx, w, q3, k3, v3,
    qb, kb, vb, ob, at3, part, e1r, e2s, e2r, tn, tb, aligned,
    pp, s1, r1, sf, rf, s2, r2, pr, stat, cosx,
    own, g1s, g1r, g2s, g2r, g3s, g3r,
    l_s, l3_s, k_s, k_r, ks_s, ks_r, v_s, v_r, vs_s, vs_r, q_s, q_r, o_s, o_r, e_s, e_r, t_s, t_r, ty_s, ty_r, tc_s, tc_r,
    p_s, p_r, st_s, st_r, c_s, c_r, a_s, a_r, g_s, g_r, x_s, x_r, z_s, z_r,
):
    dp, seq, y = lax.axis_index("dp"), lax.axis_index("seq"), lax.axis_index("head")
    x, zl, zh, c = dp // 2, dp % 2, seq // 2, seq % 2
    o = 1 - c
    odd = y % 2
    half, chunk = y // 4, y % 4
    pos = zh * 2 + zl
    at_sib = {"seq": zh * 2 + o}
    sent = []

    def at_y(d):
        return {"head": (y + d) % 8}

    def go(copy):
        copy.start()
        sent.append(copy)

    loads = [
        pltpu.make_async_copy(src, dst, l_s.at[n])
        for n, (src, dst) in enumerate(
            ((patch_h, patch), (enc_h, enc_w), (gain_h, gain), (bias_h, bias), (idx_h, idx), (w_h, w))
        )
    ]
    qkv_loads = [
        [
            pltpu.make_async_copy(src.at[:, h * HD : (h + 1) * HD], dst.at[h], l3_s.at[n, h])
            for h in range(NH)
        ]
        for n, (src, dst) in enumerate(((k_h, k3), (v_h, v3), (q_h, q3)))
    ]
    for copy in (*loads[:2], *qkv_loads[0], *qkv_loads[1], *qkv_loads[2], *loads[2:]):
        copy.start()

    barrier = pltpu.get_barrier_semaphore()
    peers = [at_y(d) for d in range(1, 8)]
    peers += [{"dp": (x + d) % 4 * 2 + zl} for d in (1, 2, 3)]
    peers += [at_sib]
    for d in range(1, 8):
        to = (pos + d) % 8
        for cc in range(2):
            peers.append({"dp": x * 2 + to % 2, "seq": to // 2 * 2 + cc})
    for peer in peers:
        pl.semaphore_signal(barrier, inc=1, device_id=peer, device_id_type=MESH)
    loads[0].wait()
    loads[1].wait()
    share = lax.dot_general(
        patch[...], enc_w[...], (((0,), (0,)), ((), ())), preferred_element_type=F32
    )
    for z in range(4):
        for cc in range(2):
            part[cc, z] = share[(2 * z + cc) * 16 : (2 * z + cc + 1) * 16]
    for group in qkv_loads:
        for copy in group:
            copy.wait()
    pl.semaphore_wait(barrier, len(peers))

    first = 2 * zl + 1
    mine_r = (zh + 4 - first) % 4
    active = mine_r < NH
    workers = [(first + r) % 4 for r in range(NH)]
    cond_sent = []

    def go_if(cond, copy):
        cond_sent.append((cond, copy))

        @pl.when(cond)
        def _():
            copy.start()

    def scatter(src, buf, ss, rs):
        for r, worker in enumerate(workers):
            go_if(worker != zh, remote(src.at[r], buf.at[seq], ss.at[r], rs.at[zh], {"seq": worker * 2 + c}))

    def to_sib(buf, ss, rs, z):
        copy = remote(buf.at[z * 2 + c], buf.at[z * 2 + c], ss.at[z], rs.at[z], at_sib)
        copy.start()
        return copy

    def keep(src, buf, ss, rs):
        @pl.when(active)
        def _():
            buf[seq] = src[mine_r]
            to_sib(buf, ss, rs, zh)

    def pass_on(buf, rs, ss2, rs2):
        @pl.when(active)
        def _():
            for d in (1, 3, 2):
                z = (zh + d) % 4
                remote(buf.at[z * 2 + c], buf.at[z * 2 + c], rs.at[z], rs.at[z], at_sib).wait_recv()
                to_sib(buf, ss2, rs2, z)

    scatter(k3, kb, k_s, k_r)
    keep(k3, kb, ks_s, ks_r)
    e1 = remote(part.at[o], e1r, e_s.at[0], e_r.at[0], at_sib)
    go(e1)
    e1.wait_recv()
    for d in (2, 1, 3):
        to = (zh + d) % 4
        e2s[d] = (part[c, to] + e1r[to]).astype(BF)
        go(remote(e2s.at[d], e2r.at[4 - d], e_s.at[d], e_r.at[4 - d], {"seq": to * 2 + c}))
    scatter(v3, vb, v_s, v_r)
    keep(v3, vb, vs_s, vs_r)
    pass_on(kb, k_r, ks_s, ks_r)
    enc = part[c, zh] + e1r[zh]
    for d in (1, 2, 3):
        remote(e2s.at[d], e2r.at[d], e_s.at[d], e_r.at[d], at_sib).wait_recv()
        enc = enc + e2r[d].astype(F32)
    loads[2].wait()
    loads[3].wait()
    average = jnp.mean(enc, axis=1, keepdims=True)
    centred = enc - average
    variance = jnp.mean(centred * centred, axis=1, keepdims=True)
    normed = (
        centred * lax.rsqrt(variance + layer_eps) * gain[...].reshape(1, E) + bias[...].reshape(1, E)
    ).astype(BF)
    for e in range(4):
        tn[e, zh] = normed[:, e * EC : (e + 1) * EC]
    for d in (2, 1, 3):
        to = (zh + d) % 4
        go(remote(tn.at[:, zh], tn.at[:, zh], t_s.at[d], t_r.at[4 - d], {"seq": to * 2 + c}))

    for i in range(PH):
        rows = slice(i * PT, (i + 1) * PT)
        for r, worker in enumerate(workers):
            go_if(
                worker != zh,
                remote(q3.at[r, rows], qb.at[i, zh], q_s.at[i, r], q_r.at[i, zh], {"seq": worker * 2 + c}),
            )
    pass_on(vb, v_r, vs_s, vs_r)
    for d in (1, 2, 3):
        fr = (zh + d) % 4
        remote(tn.at[:, fr], tn.at[:, fr], t_s.at[d], t_r.at[d], at_sib).wait_recv()
    for d in (4, 3, 5, 2, 6, 1, 7):
        go(remote(tn.at[(y + d) % 4], tb.at[y, c], ty_s.at[d], ty_r.at[8 - d], at_y(d)))
    tb[y, c] = tn[chunk]

    @pl.when(active)
    def _():
        for buf, rs in ((kb, ks_r), (vb, vs_r)):
            for z in range(4):
                remote(buf.at[z * 2 + o], buf.at[z * 2 + o], rs.at[z], rs.at[z], at_sib).wait_recv()

    def attend(i):
        rows = slice(i * PT, (i + 1) * PT)
        qb[i, zh] = q3[mine_r, rows]
        for d in (1, 3, 2):
            z = (zh + d) % 4
            remote(qb.at[i, z], qb.at[i, z], q_r.at[i, z], q_r.at[i, z], at_sib).wait_recv()
        scores = lax.dot_general(
            qb[i].reshape(4 * PT, HD), kb[...].reshape(8 * TOK, HD), (((1,), (1,)), ((), ())),
            preferred_element_type=F32,
        )
        top = jnp.max(scores, axis=1, keepdims=True)
        expo = jnp.exp2((scores - top) * EXP_SCALE).astype(BF)
        wide = jnp.concatenate([vb[...].reshape(8 * TOK, HD), jnp.ones((8 * TOK, HD), BF)], axis=1)
        out = jnp.dot(expo, wide, preferred_element_type=F32)
        ob[i] = (out[:, :HD] / out[:, HD:]).astype(BF).reshape(4, PT, HD)
        for d in (2, 1, 3):
            z = (zh + d) % 4
            remote(ob.at[i, z], at3.at[mine_r, rows], o_s.at[i, d], o_r.at[mine_r, i], {"seq": z * 2 + c}).start()
        at3[mine_r, rows] = ob[i, zh]

    @pl.when(active)
    def _():
        attend(0)
        attend(1)
        attend(2)

    def gather_start(at, ss, rs):
        for n, d in enumerate((2, 6, 1, 7)):
            go(remote(at(y), at(y), ss(n), rs(8 - d), at_y(d)))

    def gather_took(at, rs, d):
        fr = (y + d) % 8
        remote(at(fr), at(fr), rs(d), rs(d), at_y(d)).wait_recv()

    def gather_relay(at, ss, rs):
        gather_took(at, rs, 6)
        lo = (y + 6) % 8
        gather_took(at, rs, 2)
        hi = (y + 2) % 8
        far = (y + 6 + 4 * odd) % 8
        go(remote(at(far), at(far), ss(6), rs(4), at_y(2 + 4 * odd)))
        go(remote(at(lo), at(lo), ss(4), rs(5), at_y(1)))
        go(remote(at(hi), at(hi), ss(5), rs(3), at_y(7)))

    loads[5].wait()

    for i in range(PH):
        rows = slice(i * PT, (i + 1) * PT)
        for r, worker in enumerate(workers):

            @pl.when(worker != zh)
            def _(r=r, rows=rows, i=i):
                remote(at3.at[r, rows], at3.at[r, rows], o_r.at[r, i], o_r.at[r, i], at_sib).wait_recv()

        attn[rows, :] = jnp.concatenate([at3[r, rows] for r in range(NH)], axis=1)
        partial = lax.dot_general(
            attn[rows, :], w[...], (((1,), (1,)), ((), ())), preferred_element_type=F32
        )
        for t in range(2):
            for e in range(4):
                pp[i, t * 4 + e] = partial[t * SUB : (t + 1) * SUB, e * EC : (e + 1) * EC]
        sf[i] = pp[i, (y + 4) % 8].astype(BF)
        go(remote(sf.at[i], rf.at[i], p_s.at[i, 0], p_r.at[i, 0], at_y(2 + 4 * odd)))
        s1[i, 0, 1] = pp[i, (y + 3) % 8].astype(BF)
        s1[i, 0, 0] = pp[i, (y + 1) % 8].astype(BF)
        go(remote(s1.at[i, 0], r1.at[i, 0], p_s.at[i, 1], p_r.at[i, 1], at_y(1)))
        s1[i, 1, 1] = pp[i, (y + 5) % 8].astype(BF)
        s1[i, 1, 0] = pp[i, (y + 7) % 8].astype(BF)
        go(remote(s1.at[i, 1], r1.at[i, 1], p_s.at[i, 2], p_r.at[i, 2], at_y(7)))
    for i in range(PH):
        remote(sf.at[i], rf.at[i], p_s.at[i, 0], p_r.at[i, 0], at_y(1)).wait_recv()
        remote(s1.at[i, 0], r1.at[i, 0], p_s.at[i, 1], p_r.at[i, 1], at_y(1)).wait_recv()
        remote(s1.at[i, 1], r1.at[i, 1], p_s.at[i, 2], p_r.at[i, 2], at_y(7)).wait_recv()
        far = rf[i].astype(F32)
        upper = pp[i, (y + 2) % 8] + r1[i, 0, 1].astype(F32)
        lower = pp[i, (y + 6) % 8] + r1[i, 1, 1].astype(F32)
        s2[i, 0] = jnp.where(odd == 0, upper + far, upper).astype(BF)
        go(remote(s2.at[i, 0], r2.at[i, 0], p_s.at[i, 3], p_r.at[i, 3], at_y(2)))
        s2[i, 1] = jnp.where(odd == 1, lower + far, lower).astype(BF)
        go(remote(s2.at[i, 1], r2.at[i, 1], p_s.at[i, 4], p_r.at[i, 4], at_y(6)))

    for d in range(1, 8):
        fr = (y + d) % 8
        remote(tb.at[fr, c], tb.at[fr, c], ty_s.at[d], ty_r.at[d], at_y(d)).wait_recv()
    to_core = remote(tb.at[:, c], tb.at[:, c], tc_s.at[0], tc_r.at[0], at_sib)
    go(to_core)
    loads[4].wait()
    picks = idx[...]
    rest = picks % 128
    spot = picks // 128 * 128 + rest // 16 % 2 * 64 + rest // 32 * 16 + rest % 16
    hot = (lax.broadcasted_iota(jnp.int32, (1024, TOK), 0) == spot).astype(F32).astype(BF)
    remote(tb.at[:, o], tb.at[:, o], tc_s.at[0], tc_r.at[0], at_sib).wait_recv()
    aligned[...] = lax.dot_general(
        hot, tb[...].reshape(1024, EC), (((0,), (0,)), ((), ())), preferred_element_type=F32
    )

    lane = lax.broadcasted_iota(jnp.int32, (128, 128), 1)
    sub = lax.broadcasted_iota(jnp.int32, (128, 128), 0)

    def tall(column):
        return jnp.concatenate([column, jnp.zeros((128 - SUB, 1), F32)], axis=0)

    def own_rows(i):
        return pl.ds(pl.multiple_of(i * PT + half * SUB, 16), SUB)

    for i in range(PH):
        remote(s2.at[i, 0], r2.at[i, 0], p_s.at[i, 3], p_r.at[i, 3], at_y(2)).wait_recv()
        remote(s2.at[i, 1], r2.at[i, 1], p_s.at[i, 4], p_r.at[i, 4], at_y(6)).wait_recv()
        proj = (
            pp[i, y]
            + (r1[i, 0, 0].astype(F32) + r1[i, 1, 0].astype(F32))
            + (r2[i, 0].astype(F32) + r2[i, 1].astype(F32))
        )
        pp[i, y] = proj
        al = aligned[own_rows(i), :]
        sums = [jnp.sum(v, axis=1, keepdims=True) for v in (proj * proj, proj * al, al * al)]
        packed = jnp.where(
            lane == 0, tall(sums[0]), jnp.where(lane == 1, tall(sums[1]), jnp.where(lane == 2, tall(sums[2]), 0.0))
        )
        stat[i, chunk] = packed.T[0:8, :]
        for d in (2, 1, 3):
            to = half * 4 + (chunk + d) % 4
            go(remote(stat.at[i, chunk], stat.at[i, chunk], st_s.at[i, d], st_r.at[i, 4 - d], {"head": to}))

    def grad_at(i):
        return (lambda n: pr.at[i, n]), (lambda n: a_s.at[i, n]), (lambda n: a_r.at[i, n])

    for i in range(PH):
        for d in (1, 2, 3):
            fr = (chunk + d) % 4
            remote(stat.at[i, fr], stat.at[i, fr], st_s.at[i, d], st_r.at[i, d], at_sib).wait_recv()
        total = (stat[i, 0] + stat[i, 1]) + (stat[i, 2] + stat[i, 3])
        pn = jnp.sqrt(total[0:1] + cos_eps)
        an = jnp.sqrt(total[2:3] + cos_eps)
        cos = total[1:2] / (pn * an)
        cosx[0, i] = jnp.broadcast_to(cos, (8, 128))
        factors = jnp.where(sub == 0, 1.0 / (pn * an), jnp.where(sub == 1, cos / (pn * pn), 0.0)).T
        al = aligned[own_rows(i), :]
        pr[i, y] = (-(al * factors[:SUB, 0:1] - factors[:SUB, 1:2] * pp[i, y])).astype(BF)
        gather_start(*grad_at(i))
    go(remote(cosx.at[0], cosx.at[1], c_s.at[0], c_r.at[0], at_y(4)))
    for i in range(PH):
        gather_relay(*grad_at(i))
    for i in range(PH):
        at, ss, rs = grad_at(i)
        for d in (1, 7, 3, 5, 4):
            gather_took(at, rs, d)

    def grad_columns(e):
        return jnp.concatenate([pr[i, t * 4 + e] for i in range(PH) for t in range(2)], axis=0)

    xo, xu, xd = (x + 2) % 4, (x + 1) % 4, (x + 3) % 4
    for n, xx in enumerate((xo, xu, xd, x)):
        block = lax.dot_general(grad_columns(xx), attn[...], (((0,), (0,)), ((), ())), preferred_element_type=F32)
        for zz in range(2):
            own[xx, zz] = block[zz * BLK : (zz + 1) * BLK]
        g1s[n] = own[xx, o].astype(BF)
        go(remote(g1s.at[n], g1r.at[n], g_s.at[n], g_r.at[n], at_sib))
    for n, (xx, d) in enumerate(((xo, 2), (xu, 1), (xd, 3))):
        remote(g1s.at[n], g1r.at[n], g_s.at[n], g_r.at[n], at_sib).wait_recv()
        g2s[n] = (own[xx, c] + g1r[n].astype(F32)).astype(BF)
        first_rows = slice(0, HB)
        go(remote(g2s.at[n, first_rows], g2r.at[4 - d, first_rows], x_s.at[0, d], x_r.at[0, 4 - d], {"dp": xx * 2 + zl}))
    for n, (xx, d) in enumerate(((xo, 2), (xu, 1), (xd, 3))):
        last_rows = slice(HB, BLK)
        go(remote(g2s.at[n, last_rows], g2r.at[4 - d, last_rows], x_s.at[1, d], x_r.at[1, 4 - d], {"dp": xx * 2 + zl}))
    back = jnp.dot(grad_columns(0), w[:EC], preferred_element_type=F32)
    for e in range(1, 4):
        back = back + jnp.dot(grad_columns(e), w[e * EC : (e + 1) * EC], preferred_element_type=F32)
    grad_attn[...] = back.astype(BF)
    remote(g1s.at[3], g1r.at[3], g_s.at[3], g_r.at[3], at_sib).wait_recv()
    for part_of in range(2):
        rows = slice(part_of * HB, (part_of + 1) * HB)
        mine = own[x, c, rows] + g1r[3, rows].astype(F32)
        for d in (1, 3, 2):
            remote(g2s.at[0, rows], g2r.at[d, rows], x_s.at[part_of, d], x_r.at[part_of, d], at_sib).wait_recv()
            mine = mine + g2r[d, rows].astype(F32)
        for n in range(4):
            piece = jnp.concatenate([mine[n * 24 : (n + 1) * 24], jnp.zeros((8, DA), F32)], axis=0)
            g3s[part_of * 4 + n] = piece.astype(BF)
        for n in range(4):
            tz, cc = part_of * 2 + n // 2, n % 2
            go_if(
                (tz != zh) | (zl != c) | (c != cc),
                remote(g3s.at[tz * 2 + cc], g3r.at[pos], z_s.at[tz, cc], z_r.at[pos],
                       {"dp": x * 2 + c, "seq": tz * 2 + cc}),
            )
    row = jnp.zeros((8, 384), F32)
    token = lax.broadcasted_iota(jnp.int32, (8, 384), 1)
    remote(cosx.at[0], cosx.at[1], c_s.at[0], c_r.at[0], at_y(4)).wait_recv()
    for n in range(2):
        for i in range(PH):
            start = i * PT + (half + (1 - 2 * half) * n) * SUB
            wide = jnp.concatenate([cosx[n, i], jnp.zeros((8, 256), F32)], axis=1)
            inside = (token >= start) & (token < start + SUB)
            row = jnp.where(inside, pltpu.roll(wide, start, 1), row)
    cos_out[...] = row[0:1, :TOK]

    @pl.when(zl == c)
    def _():
        g3r[pos] = g3s[zh * 2 + c]

    @pl.when(zl != c)
    def _():
        remote(g3s.at[0], g3r.at[pos], z_s.at[0, 0], z_r.at[pos], at_sib).wait_recv()

    for d in range(1, 8):
        fr = (pos + d) % 8
        remote(g3s.at[0], g3r.at[fr], z_s.at[0, 0], z_r.at[fr], at_sib).wait_recv()
    total = g3r[0].astype(F32)
    for n in range(1, 8):
        total = total + g3r[n].astype(F32)
    grad_proj[...] = total[:24]

    @pl.when(active)
    def _():
        for z in range(4):
            for buf, ss in ((kb, ks_s), (vb, vs_s)):
                remote(buf.at[z * 2 + c], buf.at[z * 2 + c], ss.at[z], ks_r.at[z], at_sib).wait_send()
        for i in range(PH):
            for d in (1, 2, 3):
                remote(ob.at[i, d], at3.at[0, :PT], o_s.at[i, d], o_r.at[0, i], at_sib).wait_send()

    for cond, copy in cond_sent:

        @pl.when(cond)
        def _(copy=copy):
            copy.wait_send()

    for copy in sent:
        copy.wait_send()


def settle(a, b, c, d, a_out, b_out, c_out, d_out, a_in, b_in, c_in, d_in, sems):
    first = [
        pltpu.make_async_copy(src, dst, sems.at[n])
        for n, (src, dst) in enumerate(((a, a_in), (b, b_in), (c, c_in), (d, d_in)))
    ]
    second = [
        pltpu.make_async_copy(src, dst, sems.at[n + 4])
        for n, (src, dst) in enumerate(((a_in, a_out), (b_in, b_out), (c_in, c_out), (d_in, d_out)))
    ]
    for copy in first:
        copy.start()
    for one, two in zip(first, second):
        one.wait()
        two.start()
    for copy in second:
        copy.wait()


def on_device(patch_in, enc_weight, enc_gain, enc_bias, interp_index, queries, key_rows, value_rows, proj_weight):
    vm = pl.BlockSpec(memory_space=pltpu.VMEM)
    hbm = pl.BlockSpec(memory_space=pltpu.HBM)
    dma = pltpu.SemaphoreType.DMA
    attn, cosine, grad_attn, grad_proj = pl.pallas_call(
        kernel,
        out_shape=(
            jax.ShapeDtypeStruct((TOK, DA), BF),
            jax.ShapeDtypeStruct((1, TOK), F32),
            jax.ShapeDtypeStruct((TOK, DA), BF),
            jax.ShapeDtypeStruct((24, DA), F32),
        ),
        in_specs=[hbm] * 9,
        out_specs=(vm,) * 4,
        scratch_shapes=[
            pltpu.VMEM((192, 128), BF),
            pltpu.VMEM((192, E), BF),
            pltpu.VMEM((E,), F32),
            pltpu.VMEM((E,), F32),
            pltpu.VMEM((1, TOK), jnp.int32),
            pltpu.VMEM((E, DA), BF),
            pltpu.VMEM((NH, TOK, HD), BF),
            pltpu.VMEM((NH, TOK, HD), BF),
            pltpu.VMEM((NH, TOK, HD), BF),
            pltpu.VMEM((PH, 4, PT, HD), BF),
            pltpu.VMEM((8, TOK, HD), BF),
            pltpu.VMEM((8, TOK, HD), BF),
            pltpu.VMEM((PH, 4, PT, HD), BF),
            pltpu.VMEM((NH, TOK, HD), BF),
            pltpu.VMEM((2, 4, 16, E), F32),
            pltpu.VMEM((4, 16, E), F32),
            pltpu.VMEM((4, 16, E), BF),
            pltpu.VMEM((4, 16, E), BF),
            pltpu.VMEM((4, 4, 16, EC), BF),
            pltpu.VMEM((8, 2, 4, 16, EC), BF),
            pltpu.VMEM((TOK, EC), F32),
            pltpu.VMEM((PH, 8, SUB, EC), F32),
            pltpu.VMEM((PH, 2, 2, SUB, EC), BF),
            pltpu.VMEM((PH, 2, 2, SUB, EC), BF),
            pltpu.VMEM((PH, SUB, EC), BF),
            pltpu.VMEM((PH, SUB, EC), BF),
            pltpu.VMEM((PH, 2, SUB, EC), BF),
            pltpu.VMEM((PH, 2, SUB, EC), BF),
            pltpu.VMEM((PH, 8, SUB, EC), BF),
            pltpu.VMEM((PH, 4, 8, 128), F32),
            pltpu.VMEM((2, PH, 8, 128), F32),
            pltpu.VMEM((4, 2, BLK, DA), F32),
            pltpu.VMEM((4, BLK, DA), BF),
            pltpu.VMEM((4, BLK, DA), BF),
            pltpu.VMEM((3, BLK, DA), BF),
            pltpu.VMEM((4, BLK, DA), BF),
            pltpu.VMEM((8, 32, DA), BF),
            pltpu.VMEM((8, 32, DA), BF),
            dma((6,)),
            dma((3, NH)),
            dma((NH,)),
            dma((4,)),
            dma((4,)),
            dma((4,)),
            dma((NH,)),
            dma((4,)),
            dma((4,)),
            dma((4,)),
            dma((PH, NH)),
            dma((PH, 4)),
            dma((PH, 4)),
            dma((NH, PH)),
            dma((4,)),
            dma((4,)),
            dma((4,)),
            dma((4,)),
            dma((8,)),
            dma((8,)),
            dma((8,)),
            dma((8,)),
            dma((PH, 5)),
            dma((PH, 5)),
            dma((PH, 4)),
            dma((PH, 4)),
            dma((1,)),
            dma((1,)),
            dma((PH, 8)),
            dma((PH, 8)),
            dma((4,)),
            dma((4,)),
            dma((2, 4)),
            dma((2, 4)),
            dma((4, 2)),
            dma((8,)),
        ],
        compiler_params=pltpu.CompilerParams(
            collective_id=0, has_side_effects=True, vmem_limit_bytes=56 * 2**20
        ),
        name="whole",
    )(
        patch_in[0].T,
        enc_weight,
        enc_gain,
        enc_bias,
        interp_index,
        queries[0],
        key_rows[0],
        value_rows[0],
        proj_weight,
    )
    results = (attn, cosine, grad_attn, grad_proj)
    attn, cosine, grad_attn, grad_proj = pl.pallas_call(
        settle,
        out_shape=tuple(jax.ShapeDtypeStruct(a.shape, a.dtype) for a in results),
        in_specs=[hbm] * 4,
        out_specs=(hbm,) * 4,
        scratch_shapes=[pltpu.VMEM(a.shape, a.dtype) for a in results] + [dma((8,))],
        compiler_params=pltpu.CompilerParams(vmem_limit_bytes=60 * 2**20),
        name="settle",
    )(*results)
    return attn[None], cosine, grad_attn[None], grad_proj


def solution(mesh):
    placed = (
        P("dp", "head", "seq"),
        P("seq", None),
        P(),
        P(),
        P("dp", "seq"),
        P("dp", "seq", "head"),
        P("dp", "seq", "head"),
        P("dp", "seq", "head"),
        P(None, "head"),
    )
    return jax.shard_map(
        on_device,
        mesh=mesh,
        in_specs=placed,
        out_specs=(
            P("dp", "seq", "head"),
            P("dp", "seq"),
            P("dp", "seq", "head"),
            P(("dp", "seq"), "head"),
        ),
        check_vma=False,
    )
```

```python
import jax
import jax.numpy as jnp
from jax import lax
from jax.experimental import pallas as pl
from jax.experimental.pallas import tpu as pltpu
from jax.sharding import PartitionSpec as P

MESH = pl.DeviceIdType.MESH
BF = jnp.bfloat16
F32 = jnp.float32

E = 1536
HD = 128
NH = 3
DA = NH * HD
TOK = 288
SUB = 48
EC = 384
PH = 3
PT = 2 * SUB
HB = 48
BLK = 192

layer_eps = 1e-06
cos_eps = 1e-06
EXP_SCALE = HD**-0.5 * 1.4426950408889634


def remote(src, dst, send, recv, where):
    return pltpu.make_async_remote_copy(
        src_ref=src, dst_ref=dst, send_sem=send, recv_sem=recv, device_id=where, device_id_type=MESH
    )


def kernel(
    patch_h, enc_h, gain_h, bias_h, idx_h, q_h, k_h, v_h, w_h,
    attn, cos_out, grad_attn, grad_proj,
    patch, enc_w, gain, bias, idx, w, q3, k3, v3,
    qb, kb, vb, ob, at3, part, e1r, e2s, e2r, tn, tb, aligned,
    pp, s1, r1, sf, rf, s2, r2, pr, stat, cosx,
    own, g1s, g1r, g2s, g2r, g3s, g3r,
    l_s, l3_s, k_s, k_r, ks_s, ks_r, v_s, v_r, vs_s, vs_r, q_s, q_r, o_s, o_r, e_s, e_r, t_s, t_r, ty_s, ty_r, tc_s, tc_r,
    p_s, p_r, st_s, st_r, c_s, c_r, a_s, a_r, g_s, g_r, x_s, x_r, z_s, z_r,
):
    dp, seq, y = lax.axis_index("dp"), lax.axis_index("seq"), lax.axis_index("head")
    x, zl, zh, c = dp // 2, dp % 2, seq // 2, seq % 2
    o = 1 - c
    odd = y % 2
    half, chunk = y // 4, y % 4
    pos = zh * 2 + zl
    at_sib = {"seq": zh * 2 + o}
    sent = []

    def at_y(d):
        return {"head": (y + d) % 8}

    def go(copy):
        copy.start()
        sent.append(copy)

    loads = [
        pltpu.make_async_copy(src, dst, l_s.at[n])
        for n, (src, dst) in enumerate(
            ((patch_h, patch), (enc_h, enc_w), (gain_h, gain), (bias_h, bias), (idx_h, idx), (w_h, w))
        )
    ]
    qkv_loads = [
        [
            pltpu.make_async_copy(src.at[:, h * HD : (h + 1) * HD], dst.at[h], l3_s.at[n, h])
            for h in range(NH)
        ]
        for n, (src, dst) in enumerate(((k_h, k3), (v_h, v3), (q_h, q3)))
    ]
    for copy in (*loads[:2], *qkv_loads[0], *qkv_loads[1], *qkv_loads[2], *loads[2:]):
        copy.start()

    barrier = pltpu.get_barrier_semaphore()
    peers = [at_y(d) for d in range(1, 8)]
    peers += [{"dp": (x + d) % 4 * 2 + zl} for d in (1, 2, 3)]
    peers += [at_sib]
    for d in range(1, 8):
        to = (pos + d) % 8
        for cc in range(2):
            peers.append({"dp": x * 2 + to % 2, "seq": to // 2 * 2 + cc})
    for peer in peers:
        pl.semaphore_signal(barrier, inc=1, device_id=peer, device_id_type=MESH)
    loads[0].wait()
    loads[1].wait()
    share = lax.dot_general(
        patch[...], enc_w[...], (((0,), (0,)), ((), ())), preferred_element_type=F32
    )
    for z in range(4):
        for cc in range(2):
            part[cc, z] = share[(2 * z + cc) * 16 : (2 * z + cc + 1) * 16]
    for group in qkv_loads:
        for copy in group:
            copy.wait()
    pl.semaphore_wait(barrier, len(peers))

    first = zl + 1
    mine_r = (zh + 4 - first) % 4
    active = mine_r < NH
    workers = [(first + r) % 4 for r in range(NH)]
    cond_sent = []

    def go_if(cond, copy):
        cond_sent.append((cond, copy))

        @pl.when(cond)
        def _():
            copy.start()

    def scatter(src, buf, ss, rs):
        for r, worker in enumerate(workers):
            go_if(worker != zh, remote(src.at[r], buf.at[seq], ss.at[r], rs.at[zh], {"seq": worker * 2 + c}))

    def to_sib(buf, ss, rs, z):
        copy = remote(buf.at[z * 2 + c], buf.at[z * 2 + c], ss.at[z], rs.at[z], at_sib)
        copy.start()
        return copy

    def keep(src, buf, ss, rs):
        @pl.when(active)
        def _():
            buf[seq] = src[mine_r]
            to_sib(buf, ss, rs, zh)

    def pass_on(buf, rs, ss2, rs2):
        @pl.when(active)
        def _():
            for d in (1, 3, 2):
                z = (zh + d) % 4
                remote(buf.at[z * 2 + c], buf.at[z * 2 + c], rs.at[z], rs.at[z], at_sib).wait_recv()
                to_sib(buf, ss2, rs2, z)

    scatter(k3, kb, k_s, k_r)
    keep(k3, kb, ks_s, ks_r)
    e1 = remote(part.at[o], e1r, e_s.at[0], e_r.at[0], at_sib)
    go(e1)
    e1.wait_recv()
    for d in (2, 1, 3):
        to = (zh + d) % 4
        e2s[d] = (part[c, to] + e1r[to]).astype(BF)
        go(remote(e2s.at[d], e2r.at[4 - d], e_s.at[d], e_r.at[4 - d], {"seq": to * 2 + c}))
    scatter(v3, vb, v_s, v_r)
    keep(v3, vb, vs_s, vs_r)
    pass_on(kb, k_r, ks_s, ks_r)
    enc = part[c, zh] + e1r[zh]
    for d in (1, 2, 3):
        remote(e2s.at[d], e2r.at[d], e_s.at[d], e_r.at[d], at_sib).wait_recv()
        enc = enc + e2r[d].astype(F32)
    loads[2].wait()
    loads[3].wait()
    average = jnp.mean(enc, axis=1, keepdims=True)
    centred = enc - average
    variance = jnp.mean(centred * centred, axis=1, keepdims=True)
    normed = (
        centred * lax.rsqrt(variance + layer_eps) * gain[...].reshape(1, E) + bias[...].reshape(1, E)
    ).astype(BF)
    for e in range(4):
        tn[e, zh] = normed[:, e * EC : (e + 1) * EC]
    for d in (2, 1, 3):
        to = (zh + d) % 4
        go(remote(tn.at[:, zh], tn.at[:, zh], t_s.at[d], t_r.at[4 - d], {"seq": to * 2 + c}))

    for i in range(PH):
        rows = slice(i * PT, (i + 1) * PT)
        for r, worker in enumerate(workers):
            go_if(
                worker != zh,
                remote(q3.at[r, rows], qb.at[i, zh], q_s.at[i, r], q_r.at[i, zh], {"seq": worker * 2 + c}),
            )
    pass_on(vb, v_r, vs_s, vs_r)
    for d in (1, 2, 3):
        fr = (zh + d) % 4
        remote(tn.at[:, fr], tn.at[:, fr], t_s.at[d], t_r.at[d], at_sib).wait_recv()
    for d in (4, 3, 5, 2, 6, 1, 7):
        go(remote(tn.at[(y + d) % 4], tb.at[y, c], ty_s.at[d], ty_r.at[8 - d], at_y(d)))
    tb[y, c] = tn[chunk]

    @pl.when(active)
    def _():
        for buf, rs in ((kb, ks_r), (vb, vs_r)):
            for z in range(4):
                remote(buf.at[z * 2 + o], buf.at[z * 2 + o], rs.at[z], rs.at[z], at_sib).wait_recv()

    def attend(i):
        rows = slice(i * PT, (i + 1) * PT)
        qb[i, zh] = q3[mine_r, rows]
        for d in (1, 3, 2):
            z = (zh + d) % 4
            remote(qb.at[i, z], qb.at[i, z], q_r.at[i, z], q_r.at[i, z], at_sib).wait_recv()
        scores = lax.dot_general(
            qb[i].reshape(4 * PT, HD), kb[...].reshape(8 * TOK, HD), (((1,), (1,)), ((), ())),
            preferred_element_type=F32,
        )
        top = jnp.max(scores, axis=1, keepdims=True)
        expo = jnp.exp2((scores - top) * EXP_SCALE).astype(BF)
        wide = jnp.concatenate([vb[...].reshape(8 * TOK, HD), jnp.ones((8 * TOK, HD), BF)], axis=1)
        out = jnp.dot(expo, wide, preferred_element_type=F32)
        ob[i] = (out[:, :HD] / out[:, HD:]).astype(BF).reshape(4, PT, HD)
        for d in (2, 1, 3):
            z = (zh + d) % 4
            remote(ob.at[i, z], at3.at[mine_r, rows], o_s.at[i, d], o_r.at[mine_r, i], {"seq": z * 2 + c}).start()
        at3[mine_r, rows] = ob[i, zh]

    @pl.when(active)
    def _():
        attend(0)
        attend(1)
        attend(2)

    def gather_start(at, ss, rs):
        for n, d in enumerate((2, 6, 1, 7)):
            go(remote(at(y), at(y), ss(n), rs(8 - d), at_y(d)))

    def gather_took(at, rs, d):
        fr = (y + d) % 8
        remote(at(fr), at(fr), rs(d), rs(d), at_y(d)).wait_recv()

    def gather_relay(at, ss, rs):
        gather_took(at, rs, 6)
        lo = (y + 6) % 8
        gather_took(at, rs, 2)
        hi = (y + 2) % 8
        far = (y + 6 + 4 * odd) % 8
        go(remote(at(far), at(far), ss(6), rs(4), at_y(2 + 4 * odd)))
        go(remote(at(lo), at(lo), ss(4), rs(5), at_y(1)))
        go(remote(at(hi), at(hi), ss(5), rs(3), at_y(7)))

    loads[5].wait()

    for i in range(PH):
        rows = slice(i * PT, (i + 1) * PT)
        for r, worker in enumerate(workers):

            @pl.when(worker != zh)
            def _(r=r, rows=rows, i=i):
                remote(at3.at[r, rows], at3.at[r, rows], o_r.at[r, i], o_r.at[r, i], at_sib).wait_recv()

        attn[rows, :] = jnp.concatenate([at3[r, rows] for r in range(NH)], axis=1)
        partial = lax.dot_general(
            attn[rows, :], w[...], (((1,), (1,)), ((), ())), preferred_element_type=F32
        )
        for t in range(2):
            for e in range(4):
                pp[i, t * 4 + e] = partial[t * SUB : (t + 1) * SUB, e * EC : (e + 1) * EC]
        sf[i] = pp[i, (y + 4) % 8].astype(BF)
        go(remote(sf.at[i], rf.at[i], p_s.at[i, 0], p_r.at[i, 0], at_y(2 + 4 * odd)))
        s1[i, 0, 1] = pp[i, (y + 3) % 8].astype(BF)
        s1[i, 0, 0] = pp[i, (y + 1) % 8].astype(BF)
        go(remote(s1.at[i, 0], r1.at[i, 0], p_s.at[i, 1], p_r.at[i, 1], at_y(1)))
        s1[i, 1, 1] = pp[i, (y + 5) % 8].astype(BF)
        s1[i, 1, 0] = pp[i, (y + 7) % 8].astype(BF)
        go(remote(s1.at[i, 1], r1.at[i, 1], p_s.at[i, 2], p_r.at[i, 2], at_y(7)))
    for i in range(PH):
        remote(sf.at[i], rf.at[i], p_s.at[i, 0], p_r.at[i, 0], at_y(1)).wait_recv()
        remote(s1.at[i, 0], r1.at[i, 0], p_s.at[i, 1], p_r.at[i, 1], at_y(1)).wait_recv()
        remote(s1.at[i, 1], r1.at[i, 1], p_s.at[i, 2], p_r.at[i, 2], at_y(7)).wait_recv()
        far = rf[i].astype(F32)
        upper = pp[i, (y + 2) % 8] + r1[i, 0, 1].astype(F32)
        lower = pp[i, (y + 6) % 8] + r1[i, 1, 1].astype(F32)
        s2[i, 0] = jnp.where(odd == 0, upper + far, upper).astype(BF)
        go(remote(s2.at[i, 0], r2.at[i, 0], p_s.at[i, 3], p_r.at[i, 3], at_y(2)))
        s2[i, 1] = jnp.where(odd == 1, lower + far, lower).astype(BF)
        go(remote(s2.at[i, 1], r2.at[i, 1], p_s.at[i, 4], p_r.at[i, 4], at_y(6)))

    for d in range(1, 8):
        fr = (y + d) % 8
        remote(tb.at[fr, c], tb.at[fr, c], ty_s.at[d], ty_r.at[d], at_y(d)).wait_recv()
    to_core = remote(tb.at[:, c], tb.at[:, c], tc_s.at[0], tc_r.at[0], at_sib)
    go(to_core)
    loads[4].wait()
    picks = idx[...]
    rest = picks % 128
    spot = picks // 128 * 128 + rest // 16 % 2 * 64 + rest // 32 * 16 + rest % 16
    hot = (lax.broadcasted_iota(jnp.int32, (1024, TOK), 0) == spot).astype(F32).astype(BF)
    remote(tb.at[:, o], tb.at[:, o], tc_s.at[0], tc_r.at[0], at_sib).wait_recv()
    aligned[...] = lax.dot_general(
        hot, tb[...].reshape(1024, EC), (((0,), (0,)), ((), ())), preferred_element_type=F32
    )

    lane = lax.broadcasted_iota(jnp.int32, (128, 128), 1)
    sub = lax.broadcasted_iota(jnp.int32, (128, 128), 0)

    def tall(column):
        return jnp.concatenate([column, jnp.zeros((128 - SUB, 1), F32)], axis=0)

    def own_rows(i):
        return pl.ds(pl.multiple_of(i * PT + half * SUB, 16), SUB)

    for i in range(PH):
        remote(s2.at[i, 0], r2.at[i, 0], p_s.at[i, 3], p_r.at[i, 3], at_y(2)).wait_recv()
        remote(s2.at[i, 1], r2.at[i, 1], p_s.at[i, 4], p_r.at[i, 4], at_y(6)).wait_recv()
        proj = (
            pp[i, y]
            + (r1[i, 0, 0].astype(F32) + r1[i, 1, 0].astype(F32))
            + (r2[i, 0].astype(F32) + r2[i, 1].astype(F32))
        )
        pp[i, y] = proj
        al = aligned[own_rows(i), :]
        sums = [jnp.sum(v, axis=1, keepdims=True) for v in (proj * proj, proj * al, al * al)]
        packed = jnp.where(
            lane == 0, tall(sums[0]), jnp.where(lane == 1, tall(sums[1]), jnp.where(lane == 2, tall(sums[2]), 0.0))
        )
        stat[i, chunk] = packed.T[0:8, :]
        for d in (2, 1, 3):
            to = half * 4 + (chunk + d) % 4
            go(remote(stat.at[i, chunk], stat.at[i, chunk], st_s.at[i, d], st_r.at[i, 4 - d], {"head": to}))

    def grad_at(i):
        return (lambda n: pr.at[i, n]), (lambda n: a_s.at[i, n]), (lambda n: a_r.at[i, n])

    for i in range(PH):
        for d in (1, 2, 3):
            fr = (chunk + d) % 4
            remote(stat.at[i, fr], stat.at[i, fr], st_s.at[i, d], st_r.at[i, d], at_sib).wait_recv()
        total = (stat[i, 0] + stat[i, 1]) + (stat[i, 2] + stat[i, 3])
        pn = jnp.sqrt(total[0:1] + cos_eps)
        an = jnp.sqrt(total[2:3] + cos_eps)
        cos = total[1:2] / (pn * an)
        cosx[0, i] = jnp.broadcast_to(cos, (8, 128))
        factors = jnp.where(sub == 0, 1.0 / (pn * an), jnp.where(sub == 1, cos / (pn * pn), 0.0)).T
        al = aligned[own_rows(i), :]
        pr[i, y] = (-(al * factors[:SUB, 0:1] - factors[:SUB, 1:2] * pp[i, y])).astype(BF)
        gather_start(*grad_at(i))
    go(remote(cosx.at[0], cosx.at[1], c_s.at[0], c_r.at[0], at_y(4)))
    for i in range(PH):
        gather_relay(*grad_at(i))
    for i in range(PH):
        at, ss, rs = grad_at(i)
        for d in (1, 7, 3, 5, 4):
            gather_took(at, rs, d)

    def grad_columns(e):
        return jnp.concatenate([pr[i, t * 4 + e] for i in range(PH) for t in range(2)], axis=0)

    xo, xu, xd = (x + 2) % 4, (x + 1) % 4, (x + 3) % 4
    for n, xx in enumerate((xo, xu, xd, x)):
        block = lax.dot_general(grad_columns(xx), attn[...], (((0,), (0,)), ((), ())), preferred_element_type=F32)
        for zz in range(2):
            own[xx, zz] = block[zz * BLK : (zz + 1) * BLK]
        g1s[n] = own[xx, o].astype(BF)
        go(remote(g1s.at[n], g1r.at[n], g_s.at[n], g_r.at[n], at_sib))
    for n, (xx, d) in enumerate(((xo, 2), (xu, 1), (xd, 3))):
        remote(g1s.at[n], g1r.at[n], g_s.at[n], g_r.at[n], at_sib).wait_recv()
        g2s[n] = (own[xx, c] + g1r[n].astype(F32)).astype(BF)
        rows = slice(0, HB)
        go(remote(g2s.at[n, rows], g2r.at[4 - d, rows], x_s.at[0, d], x_r.at[0, 4 - d], {"dp": xx * 2 + zl}))
    for part_of in range(1, 4):
        for n, (xx, d) in enumerate(((xo, 2), (xu, 1), (xd, 3))):
            rows = slice(part_of * HB, (part_of + 1) * HB)
            go(
                remote(g2s.at[n, rows], g2r.at[4 - d, rows], x_s.at[part_of, d], x_r.at[part_of, 4 - d],
                       {"dp": xx * 2 + zl})
            )
    back = jnp.dot(grad_columns(0), w[:EC], preferred_element_type=F32)
    for e in range(1, 4):
        back = back + jnp.dot(grad_columns(e), w[e * EC : (e + 1) * EC], preferred_element_type=F32)
    grad_attn[...] = back.astype(BF)
    remote(g1s.at[3], g1r.at[3], g_s.at[3], g_r.at[3], at_sib).wait_recv()
    for part_of in range(4):
        rows = slice(part_of * HB, (part_of + 1) * HB)
        mine = own[x, c, rows] + g1r[3, rows].astype(F32)
        for d in (1, 3, 2):
            remote(g2s.at[0, rows], g2r.at[d, rows], x_s.at[part_of, d], x_r.at[part_of, d], at_sib).wait_recv()
            mine = mine + g2r[d, rows].astype(F32)
        for n in range(2):
            piece = jnp.concatenate([mine[n * 24 : (n + 1) * 24], jnp.zeros((8, DA), F32)], axis=0)
            g3s[part_of * 2 + n] = piece.astype(BF)
        for n in range(2):
            tz, cc = part_of, n
            go_if(
                (tz != zh) | (zl != c) | (c != cc),
                remote(g3s.at[tz * 2 + cc], g3r.at[pos], z_s.at[tz, cc], z_r.at[pos],
                       {"dp": x * 2 + c, "seq": tz * 2 + cc}),
            )
    row = jnp.zeros((8, 384), F32)
    token = lax.broadcasted_iota(jnp.int32, (8, 384), 1)
    remote(cosx.at[0], cosx.at[1], c_s.at[0], c_r.at[0], at_y(4)).wait_recv()
    for n in range(2):
        for i in range(PH):
            start = i * PT + (half + (1 - 2 * half) * n) * SUB
            wide = jnp.concatenate([cosx[n, i], jnp.zeros((8, 256), F32)], axis=1)
            inside = (token >= start) & (token < start + SUB)
            row = jnp.where(inside, pltpu.roll(wide, start, 1), row)
    cos_out[...] = row[0:1, :TOK]

    @pl.when(zl == c)
    def _():
        g3r[pos] = g3s[zh * 2 + c]

    @pl.when(zl != c)
    def _():
        remote(g3s.at[0], g3r.at[pos], z_s.at[0, 0], z_r.at[pos], at_sib).wait_recv()

    for d in range(1, 8):
        fr = (pos + d) % 8
        remote(g3s.at[0], g3r.at[fr], z_s.at[0, 0], z_r.at[fr], at_sib).wait_recv()
    total = g3r[0].astype(F32)
    for n in range(1, 8):
        total = total + g3r[n].astype(F32)
    grad_proj[...] = total[:24]

    @pl.when(active)
    def _():
        for z in range(4):
            for buf, ss in ((kb, ks_s), (vb, vs_s)):
                remote(buf.at[z * 2 + c], buf.at[z * 2 + c], ss.at[z], ks_r.at[z], at_sib).wait_send()
        for i in range(PH):
            for d in (1, 2, 3):
                remote(ob.at[i, d], at3.at[0, :PT], o_s.at[i, d], o_r.at[0, i], at_sib).wait_send()

    for cond, copy in cond_sent:

        @pl.when(cond)
        def _(copy=copy):
            copy.wait_send()

    for copy in sent:
        copy.wait_send()


def settle(a, b, c, d, a_out, b_out, c_out, d_out, a_in, b_in, c_in, d_in, sems):
    first = [
        pltpu.make_async_copy(src, dst, sems.at[n])
        for n, (src, dst) in enumerate(((a, a_in), (b, b_in), (c, c_in), (d, d_in)))
    ]
    second = [
        pltpu.make_async_copy(src, dst, sems.at[n + 4])
        for n, (src, dst) in enumerate(((a_in, a_out), (b_in, b_out), (c_in, c_out), (d_in, d_out)))
    ]
    for copy in first:
        copy.start()
    for one, two in zip(first, second):
        one.wait()
        two.start()
    for copy in second:
        copy.wait()


def on_device(patch_in, enc_weight, enc_gain, enc_bias, interp_index, queries, key_rows, value_rows, proj_weight):
    vm = pl.BlockSpec(memory_space=pltpu.VMEM)
    hbm = pl.BlockSpec(memory_space=pltpu.HBM)
    dma = pltpu.SemaphoreType.DMA
    attn, cosine, grad_attn, grad_proj = pl.pallas_call(
        kernel,
        out_shape=(
            jax.ShapeDtypeStruct((TOK, DA), BF),
            jax.ShapeDtypeStruct((1, TOK), F32),
            jax.ShapeDtypeStruct((TOK, DA), BF),
            jax.ShapeDtypeStruct((24, DA), F32),
        ),
        in_specs=[hbm] * 9,
        out_specs=(vm,) * 4,
        scratch_shapes=[
            pltpu.VMEM((192, 128), BF),
            pltpu.VMEM((192, E), BF),
            pltpu.VMEM((E,), F32),
            pltpu.VMEM((E,), F32),
            pltpu.VMEM((1, TOK), jnp.int32),
            pltpu.VMEM((E, DA), BF),
            pltpu.VMEM((NH, TOK, HD), BF),
            pltpu.VMEM((NH, TOK, HD), BF),
            pltpu.VMEM((NH, TOK, HD), BF),
            pltpu.VMEM((PH, 4, PT, HD), BF),
            pltpu.VMEM((8, TOK, HD), BF),
            pltpu.VMEM((8, TOK, HD), BF),
            pltpu.VMEM((PH, 4, PT, HD), BF),
            pltpu.VMEM((NH, TOK, HD), BF),
            pltpu.VMEM((2, 4, 16, E), F32),
            pltpu.VMEM((4, 16, E), F32),
            pltpu.VMEM((4, 16, E), BF),
            pltpu.VMEM((4, 16, E), BF),
            pltpu.VMEM((4, 4, 16, EC), BF),
            pltpu.VMEM((8, 2, 4, 16, EC), BF),
            pltpu.VMEM((TOK, EC), F32),
            pltpu.VMEM((PH, 8, SUB, EC), F32),
            pltpu.VMEM((PH, 2, 2, SUB, EC), BF),
            pltpu.VMEM((PH, 2, 2, SUB, EC), BF),
            pltpu.VMEM((PH, SUB, EC), BF),
            pltpu.VMEM((PH, SUB, EC), BF),
            pltpu.VMEM((PH, 2, SUB, EC), BF),
            pltpu.VMEM((PH, 2, SUB, EC), BF),
            pltpu.VMEM((PH, 8, SUB, EC), BF),
            pltpu.VMEM((PH, 4, 8, 128), F32),
            pltpu.VMEM((2, PH, 8, 128), F32),
            pltpu.VMEM((4, 2, BLK, DA), F32),
            pltpu.VMEM((4, BLK, DA), BF),
            pltpu.VMEM((4, BLK, DA), BF),
            pltpu.VMEM((3, BLK, DA), BF),
            pltpu.VMEM((4, BLK, DA), BF),
            pltpu.VMEM((8, 32, DA), BF),
            pltpu.VMEM((8, 32, DA), BF),
            dma((6,)),
            dma((3, NH)),
            dma((NH,)),
            dma((4,)),
            dma((4,)),
            dma((4,)),
            dma((NH,)),
            dma((4,)),
            dma((4,)),
            dma((4,)),
            dma((PH, NH)),
            dma((PH, 4)),
            dma((PH, 4)),
            dma((NH, PH)),
            dma((4,)),
            dma((4,)),
            dma((4,)),
            dma((4,)),
            dma((8,)),
            dma((8,)),
            dma((8,)),
            dma((8,)),
            dma((PH, 5)),
            dma((PH, 5)),
            dma((PH, 4)),
            dma((PH, 4)),
            dma((1,)),
            dma((1,)),
            dma((PH, 8)),
            dma((PH, 8)),
            dma((4,)),
            dma((4,)),
            dma((4, 4)),
            dma((4, 4)),
            dma((4, 2)),
            dma((8,)),
        ],
        compiler_params=pltpu.CompilerParams(
            collective_id=0, has_side_effects=True, vmem_limit_bytes=56 * 2**20
        ),
        name="whole",
    )(
        patch_in[0].T,
        enc_weight,
        enc_gain,
        enc_bias,
        interp_index,
        queries[0],
        key_rows[0],
        value_rows[0],
        proj_weight,
    )
    results = (attn, cosine, grad_attn, grad_proj)
    attn, cosine, grad_attn, grad_proj = pl.pallas_call(
        settle,
        out_shape=tuple(jax.ShapeDtypeStruct(a.shape, a.dtype) for a in results),
        in_specs=[hbm] * 4,
        out_specs=(hbm,) * 4,
        scratch_shapes=[pltpu.VMEM(a.shape, a.dtype) for a in results] + [dma((8,))],
        compiler_params=pltpu.CompilerParams(vmem_limit_bytes=60 * 2**20),
        name="settle",
    )(*results)
    return attn[None], cosine, grad_attn[None], grad_proj


def solution(mesh):
    placed = (
        P("dp", "head", "seq"),
        P("seq", None),
        P(),
        P(),
        P("dp", "seq"),
        P("dp", "seq", "head"),
        P("dp", "seq", "head"),
        P("dp", "seq", "head"),
        P(None, "head"),
    )
    return jax.shard_map(
        on_device,
        mesh=mesh,
        in_specs=placed,
        out_specs=(
            P("dp", "seq", "head"),
            P("dp", "seq"),
            P("dp", "seq", "head"),
            P(("dp", "seq"), "head"),
        ),
        check_vma=False,
    )
```

```python
import jax
import jax.numpy as jnp
from jax import lax
from jax.experimental import pallas as pl
from jax.experimental.pallas import tpu as pltpu
from jax.sharding import PartitionSpec as P

MESH = pl.DeviceIdType.MESH
BF = jnp.bfloat16
F32 = jnp.float32

E = 1536
HD = 128
NH = 3
DA = NH * HD
TOK = 288
SUB = 48
EC = 384
PH = 3
PT = 2 * SUB
HB = 48
BLK = 192

layer_eps = 1e-06
cos_eps = 1e-06
EXP_SCALE = HD**-0.5 * 1.4426950408889634


def remote(src, dst, send, recv, where):
    return pltpu.make_async_remote_copy(
        src_ref=src, dst_ref=dst, send_sem=send, recv_sem=recv, device_id=where, device_id_type=MESH
    )


def kernel(
    patch_h, enc_h, gain_h, bias_h, idx_h, q_h, k_h, v_h, w_h,
    attn, cos_out, grad_attn, grad_proj,
    patch, enc_w, gain, bias, idx, w, q3, k3, v3,
    qb, kb, vb, ob, at3, part, e1r, e2s, e2r, tn, tb, aligned,
    pp, s1, r1, sf, rf, s2, r2, pr, stat, cosx,
    own, g1s, g1r, g2s, g2r, g3s, g3r,
    l_s, l3_s, k_s, k_r, ks_s, ks_r, v_s, v_r, vs_s, vs_r, q_s, q_r, o_s, o_r, e_s, e_r, t_s, t_r, ty_s, ty_r, tc_s, tc_r,
    p_s, p_r, st_s, st_r, c_s, c_r, a_s, a_r, g_s, g_r, x_s, x_r, z_s, z_r,
):
    dp, seq, y = lax.axis_index("dp"), lax.axis_index("seq"), lax.axis_index("head")
    x, zl, zh, c = dp // 2, dp % 2, seq // 2, seq % 2
    o = 1 - c
    odd = y % 2
    half, chunk = y // 4, y % 4
    pos = zh * 2 + zl
    at_sib = {"seq": zh * 2 + o}
    sent = []

    def at_y(d):
        return {"head": (y + d) % 8}

    def go(copy):
        copy.start()
        sent.append(copy)

    loads = [
        pltpu.make_async_copy(src, dst, l_s.at[n])
        for n, (src, dst) in enumerate(
            ((patch_h, patch), (enc_h, enc_w), (gain_h, gain), (bias_h, bias), (idx_h, idx), (w_h, w))
        )
    ]
    qkv_loads = [
        [
            pltpu.make_async_copy(src.at[:, h * HD : (h + 1) * HD], dst.at[h], l3_s.at[n, h])
            for h in range(NH)
        ]
        for n, (src, dst) in enumerate(((k_h, k3), (v_h, v3), (q_h, q3)))
    ]
    for copy in (*loads[:2], *qkv_loads[0], *qkv_loads[1], *qkv_loads[2], *loads[2:]):
        copy.start()

    barrier = pltpu.get_barrier_semaphore()
    peers = [at_y(d) for d in range(1, 8)]
    peers += [{"dp": (x + d) % 4 * 2 + zl} for d in (1, 2, 3)]
    peers += [at_sib]
    for d in range(1, 8):
        to = (pos + d) % 8
        for cc in range(2):
            peers.append({"dp": x * 2 + to % 2, "seq": to // 2 * 2 + cc})
    for peer in peers:
        pl.semaphore_signal(barrier, inc=1, device_id=peer, device_id_type=MESH)
    loads[0].wait()
    loads[1].wait()
    share = lax.dot_general(
        patch[...], enc_w[...], (((0,), (0,)), ((), ())), preferred_element_type=F32
    )
    for z in range(4):
        for cc in range(2):
            part[cc, z] = share[(2 * z + cc) * 16 : (2 * z + cc + 1) * 16]
    for group in qkv_loads:
        for copy in group:
            copy.wait()
    pl.semaphore_wait(barrier, len(peers))

    first = zl + 1
    mine_r = (zh + 4 - first) % 4
    active = mine_r < NH
    workers = [(first + r) % 4 for r in range(NH)]
    cond_sent = []

    def go_if(cond, copy):
        cond_sent.append((cond, copy))

        @pl.when(cond)
        def _():
            copy.start()

    def scatter(src, buf, ss, rs):
        for r, worker in enumerate(workers):
            go_if(worker != zh, remote(src.at[r], buf.at[seq], ss.at[r], rs.at[zh], {"seq": worker * 2 + c}))

    def to_sib(buf, ss, rs, z):
        copy = remote(buf.at[z * 2 + c], buf.at[z * 2 + c], ss.at[z], rs.at[z], at_sib)
        copy.start()
        return copy

    def keep(src, buf, ss, rs):
        @pl.when(active)
        def _():
            buf[seq] = src[mine_r]
            to_sib(buf, ss, rs, zh)

    def pass_on(buf, rs, ss2, rs2):
        @pl.when(active)
        def _():
            for d in (1, 3, 2):
                z = (zh + d) % 4
                remote(buf.at[z * 2 + c], buf.at[z * 2 + c], rs.at[z], rs.at[z], at_sib).wait_recv()
                to_sib(buf, ss2, rs2, z)

    scatter(k3, kb, k_s, k_r)
    scatter(v3, vb, v_s, v_r)
    keep(k3, kb, ks_s, ks_r)
    e1 = remote(part.at[o], e1r, e_s.at[0], e_r.at[0], at_sib)
    go(e1)
    e1.wait_recv()
    for d in (2, 1, 3):
        to = (zh + d) % 4
        e2s[d] = (part[c, to] + e1r[to]).astype(BF)
        go(remote(e2s.at[d], e2r.at[4 - d], e_s.at[d], e_r.at[4 - d], {"seq": to * 2 + c}))
    keep(v3, vb, vs_s, vs_r)
    pass_on(kb, k_r, ks_s, ks_r)
    enc = part[c, zh] + e1r[zh]
    for d in (1, 2, 3):
        remote(e2s.at[d], e2r.at[d], e_s.at[d], e_r.at[d], at_sib).wait_recv()
        enc = enc + e2r[d].astype(F32)
    loads[2].wait()
    loads[3].wait()
    average = jnp.mean(enc, axis=1, keepdims=True)
    centred = enc - average
    variance = jnp.mean(centred * centred, axis=1, keepdims=True)
    normed = (
        centred * lax.rsqrt(variance + layer_eps) * gain[...].reshape(1, E) + bias[...].reshape(1, E)
    ).astype(BF)
    for e in range(4):
        tn[e, zh] = normed[:, e * EC : (e + 1) * EC]
    for d in (2, 1, 3):
        to = (zh + d) % 4
        go(remote(tn.at[:, zh], tn.at[:, zh], t_s.at[d], t_r.at[4 - d], {"seq": to * 2 + c}))

    for i in range(PH):
        rows = slice(i * PT, (i + 1) * PT)
        for r, worker in enumerate(workers):
            go_if(
                worker != zh,
                remote(q3.at[r, rows], qb.at[i, zh], q_s.at[i, r], q_r.at[i, zh], {"seq": worker * 2 + c}),
            )
    pass_on(vb, v_r, vs_s, vs_r)
    for d in (1, 2, 3):
        fr = (zh + d) % 4
        remote(tn.at[:, fr], tn.at[:, fr], t_s.at[d], t_r.at[d], at_sib).wait_recv()
    for d in (4, 3, 5, 2, 6, 1, 7):
        go(remote(tn.at[(y + d) % 4], tb.at[y, c], ty_s.at[d], ty_r.at[8 - d], at_y(d)))
    tb[y, c] = tn[chunk]

    @pl.when(active)
    def _():
        for buf, rs in ((kb, ks_r), (vb, vs_r)):
            for z in range(4):
                remote(buf.at[z * 2 + o], buf.at[z * 2 + o], rs.at[z], rs.at[z], at_sib).wait_recv()

    def attend(i):
        rows = slice(i * PT, (i + 1) * PT)
        qb[i, zh] = q3[mine_r, rows]
        for d in (1, 3, 2):
            z = (zh + d) % 4
            remote(qb.at[i, z], qb.at[i, z], q_r.at[i, z], q_r.at[i, z], at_sib).wait_recv()
        scores = lax.dot_general(
            qb[i].reshape(4 * PT, HD), kb[...].reshape(8 * TOK, HD), (((1,), (1,)), ((), ())),
            preferred_element_type=F32,
        )
        top = jnp.max(scores, axis=1, keepdims=True)
        expo = jnp.exp2((scores - top) * EXP_SCALE).astype(BF)
        wide = jnp.concatenate([vb[...].reshape(8 * TOK, HD), jnp.ones((8 * TOK, HD), BF)], axis=1)
        out = jnp.dot(expo, wide, preferred_element_type=F32)
        ob[i] = (out[:, :HD] / out[:, HD:]).astype(BF).reshape(4, PT, HD)
        for d in (2, 1, 3):
            z = (zh + d) % 4
            remote(ob.at[i, z], at3.at[mine_r, rows], o_s.at[i, d], o_r.at[mine_r, i], {"seq": z * 2 + c}).start()
        at3[mine_r, rows] = ob[i, zh]

    @pl.when(active)
    def _():
        attend(0)
        attend(1)
        attend(2)

    def gather_start(at, ss, rs):
        for n, d in enumerate((2, 6, 1, 7)):
            go(remote(at(y), at(y), ss(n), rs(8 - d), at_y(d)))

    def gather_took(at, rs, d):
        fr = (y + d) % 8
        remote(at(fr), at(fr), rs(d), rs(d), at_y(d)).wait_recv()

    def gather_relay(at, ss, rs):
        gather_took(at, rs, 6)
        lo = (y + 6) % 8
        gather_took(at, rs, 2)
        hi = (y + 2) % 8
        far = (y + 6 + 4 * odd) % 8
        go(remote(at(far), at(far), ss(6), rs(4), at_y(2 + 4 * odd)))
        go(remote(at(lo), at(lo), ss(4), rs(5), at_y(1)))
        go(remote(at(hi), at(hi), ss(5), rs(3), at_y(7)))

    loads[5].wait()

    for i in range(PH):
        rows = slice(i * PT, (i + 1) * PT)
        for r, worker in enumerate(workers):

            @pl.when(worker != zh)
            def _(r=r, rows=rows, i=i):
                remote(at3.at[r, rows], at3.at[r, rows], o_r.at[r, i], o_r.at[r, i], at_sib).wait_recv()

        attn[rows, :] = jnp.concatenate([at3[r, rows] for r in range(NH)], axis=1)
        partial = lax.dot_general(
            attn[rows, :], w[...], (((1,), (1,)), ((), ())), preferred_element_type=F32
        )
        for t in range(2):
            for e in range(4):
                pp[i, t * 4 + e] = partial[t * SUB : (t + 1) * SUB, e * EC : (e + 1) * EC]
        sf[i] = pp[i, (y + 4) % 8].astype(BF)
        go(remote(sf.at[i], rf.at[i], p_s.at[i, 0], p_r.at[i, 0], at_y(2 + 4 * odd)))
        s1[i, 0, 1] = pp[i, (y + 3) % 8].astype(BF)
        s1[i, 0, 0] = pp[i, (y + 1) % 8].astype(BF)
        go(remote(s1.at[i, 0], r1.at[i, 0], p_s.at[i, 1], p_r.at[i, 1], at_y(1)))
        s1[i, 1, 1] = pp[i, (y + 5) % 8].astype(BF)
        s1[i, 1, 0] = pp[i, (y + 7) % 8].astype(BF)
        go(remote(s1.at[i, 1], r1.at[i, 1], p_s.at[i, 2], p_r.at[i, 2], at_y(7)))
    for i in range(PH):
        remote(sf.at[i], rf.at[i], p_s.at[i, 0], p_r.at[i, 0], at_y(1)).wait_recv()
        remote(s1.at[i, 0], r1.at[i, 0], p_s.at[i, 1], p_r.at[i, 1], at_y(1)).wait_recv()
        remote(s1.at[i, 1], r1.at[i, 1], p_s.at[i, 2], p_r.at[i, 2], at_y(7)).wait_recv()
        far = rf[i].astype(F32)
        upper = pp[i, (y + 2) % 8] + r1[i, 0, 1].astype(F32)
        lower = pp[i, (y + 6) % 8] + r1[i, 1, 1].astype(F32)
        s2[i, 0] = jnp.where(odd == 0, upper + far, upper).astype(BF)
        go(remote(s2.at[i, 0], r2.at[i, 0], p_s.at[i, 3], p_r.at[i, 3], at_y(2)))
        s2[i, 1] = jnp.where(odd == 1, lower + far, lower).astype(BF)
        go(remote(s2.at[i, 1], r2.at[i, 1], p_s.at[i, 4], p_r.at[i, 4], at_y(6)))

    for d in range(1, 8):
        fr = (y + d) % 8
        remote(tb.at[fr, c], tb.at[fr, c], ty_s.at[d], ty_r.at[d], at_y(d)).wait_recv()
    to_core = remote(tb.at[:, c], tb.at[:, c], tc_s.at[0], tc_r.at[0], at_sib)
    go(to_core)
    loads[4].wait()
    picks = idx[...]
    rest = picks % 128
    spot = picks // 128 * 128 + rest // 16 % 2 * 64 + rest // 32 * 16 + rest % 16
    hot = (lax.broadcasted_iota(jnp.int32, (1024, TOK), 0) == spot).astype(F32).astype(BF)
    remote(tb.at[:, o], tb.at[:, o], tc_s.at[0], tc_r.at[0], at_sib).wait_recv()
    aligned[...] = lax.dot_general(
        hot, tb[...].reshape(1024, EC), (((0,), (0,)), ((), ())), preferred_element_type=F32
    )

    lane = lax.broadcasted_iota(jnp.int32, (128, 128), 1)
    sub = lax.broadcasted_iota(jnp.int32, (128, 128), 0)

    def tall(column):
        return jnp.concatenate([column, jnp.zeros((128 - SUB, 1), F32)], axis=0)

    def own_rows(i):
        return pl.ds(pl.multiple_of(i * PT + half * SUB, 16), SUB)

    for i in range(PH):
        remote(s2.at[i, 0], r2.at[i, 0], p_s.at[i, 3], p_r.at[i, 3], at_y(2)).wait_recv()
        remote(s2.at[i, 1], r2.at[i, 1], p_s.at[i, 4], p_r.at[i, 4], at_y(6)).wait_recv()
        proj = (
            pp[i, y]
            + (r1[i, 0, 0].astype(F32) + r1[i, 1, 0].astype(F32))
            + (r2[i, 0].astype(F32) + r2[i, 1].astype(F32))
        )
        pp[i, y] = proj
        al = aligned[own_rows(i), :]
        sums = [jnp.sum(v, axis=1, keepdims=True) for v in (proj * proj, proj * al, al * al)]
        packed = jnp.where(
            lane == 0, tall(sums[0]), jnp.where(lane == 1, tall(sums[1]), jnp.where(lane == 2, tall(sums[2]), 0.0))
        )
        stat[i, chunk] = packed.T[0:8, :]
        for d in (2, 1, 3):
            to = half * 4 + (chunk + d) % 4
            go(remote(stat.at[i, chunk], stat.at[i, chunk], st_s.at[i, d], st_r.at[i, 4 - d], {"head": to}))

    def grad_at(i):
        return (lambda n: pr.at[i, n]), (lambda n: a_s.at[i, n]), (lambda n: a_r.at[i, n])

    for i in range(PH):
        for d in (1, 2, 3):
            fr = (chunk + d) % 4
            remote(stat.at[i, fr], stat.at[i, fr], st_s.at[i, d], st_r.at[i, d], at_sib).wait_recv()
        total = (stat[i, 0] + stat[i, 1]) + (stat[i, 2] + stat[i, 3])
        pn = jnp.sqrt(total[0:1] + cos_eps)
        an = jnp.sqrt(total[2:3] + cos_eps)
        cos = total[1:2] / (pn * an)
        cosx[0, i] = jnp.broadcast_to(cos, (8, 128))
        factors = jnp.where(sub == 0, 1.0 / (pn * an), jnp.where(sub == 1, cos / (pn * pn), 0.0)).T
        al = aligned[own_rows(i), :]
        pr[i, y] = (-(al * factors[:SUB, 0:1] - factors[:SUB, 1:2] * pp[i, y])).astype(BF)
        gather_start(*grad_at(i))
    go(remote(cosx.at[0], cosx.at[1], c_s.at[0], c_r.at[0], at_y(4)))
    for i in range(PH):
        gather_relay(*grad_at(i))
    for i in range(PH):
        at, ss, rs = grad_at(i)
        for d in (1, 7, 3, 5, 4):
            gather_took(at, rs, d)

    def grad_columns(e):
        return jnp.concatenate([pr[i, t * 4 + e] for i in range(PH) for t in range(2)], axis=0)

    xo, xu, xd = (x + 2) % 4, (x + 1) % 4, (x + 3) % 4
    for n, xx in enumerate((xo, xu, xd, x)):
        block = lax.dot_general(grad_columns(xx), attn[...], (((0,), (0,)), ((), ())), preferred_element_type=F32)
        for zz in range(2):
            own[xx, zz] = block[zz * BLK : (zz + 1) * BLK]
        g1s[n] = own[xx, o].astype(BF)
        go(remote(g1s.at[n], g1r.at[n], g_s.at[n], g_r.at[n], at_sib))
    for n, (xx, d) in enumerate(((xo, 2), (xu, 1), (xd, 3))):
        remote(g1s.at[n], g1r.at[n], g_s.at[n], g_r.at[n], at_sib).wait_recv()
        g2s[n] = (own[xx, c] + g1r[n].astype(F32)).astype(BF)
        rows = slice(0, HB)
        go(remote(g2s.at[n, rows], g2r.at[4 - d, rows], x_s.at[0, d], x_r.at[0, 4 - d], {"dp": xx * 2 + zl}))
    for part_of in range(1, 4):
        for n, (xx, d) in enumerate(((xo, 2), (xu, 1), (xd, 3))):
            rows = slice(part_of * HB, (part_of + 1) * HB)
            go(
                remote(g2s.at[n, rows], g2r.at[4 - d, rows], x_s.at[part_of, d], x_r.at[part_of, 4 - d],
                       {"dp": xx * 2 + zl})
            )
    back = jnp.dot(grad_columns(0), w[:EC], preferred_element_type=F32)
    for e in range(1, 4):
        back = back + jnp.dot(grad_columns(e), w[e * EC : (e + 1) * EC], preferred_element_type=F32)
    grad_attn[...] = back.astype(BF)
    remote(g1s.at[3], g1r.at[3], g_s.at[3], g_r.at[3], at_sib).wait_recv()
    for part_of in range(4):
        rows = slice(part_of * HB, (part_of + 1) * HB)
        mine = own[x, c, rows] + g1r[3, rows].astype(F32)
        for d in (1, 3, 2):
            remote(g2s.at[0, rows], g2r.at[d, rows], x_s.at[part_of, d], x_r.at[part_of, d], at_sib).wait_recv()
            mine = mine + g2r[d, rows].astype(F32)
        for n in range(2):
            piece = jnp.concatenate([mine[n * 24 : (n + 1) * 24], jnp.zeros((8, DA), F32)], axis=0)
            g3s[part_of * 2 + n] = piece.astype(BF)
        for n in range(2):
            tz, cc = part_of, n
            go_if(
                (tz != zh) | (zl != c) | (c != cc),
                remote(g3s.at[tz * 2 + cc], g3r.at[pos], z_s.at[tz, cc], z_r.at[pos],
                       {"dp": x * 2 + c, "seq": tz * 2 + cc}),
            )
    row = jnp.zeros((8, 384), F32)
    token = lax.broadcasted_iota(jnp.int32, (8, 384), 1)
    remote(cosx.at[0], cosx.at[1], c_s.at[0], c_r.at[0], at_y(4)).wait_recv()
    for n in range(2):
        for i in range(PH):
            start = i * PT + (half + (1 - 2 * half) * n) * SUB
            wide = jnp.concatenate([cosx[n, i], jnp.zeros((8, 256), F32)], axis=1)
            inside = (token >= start) & (token < start + SUB)
            row = jnp.where(inside, pltpu.roll(wide, start, 1), row)
    cos_out[...] = row[0:1, :TOK]

    @pl.when(zl == c)
    def _():
        g3r[pos] = g3s[zh * 2 + c]

    @pl.when(zl != c)
    def _():
        remote(g3s.at[0], g3r.at[pos], z_s.at[0, 0], z_r.at[pos], at_sib).wait_recv()

    for d in range(1, 8):
        fr = (pos + d) % 8
        remote(g3s.at[0], g3r.at[fr], z_s.at[0, 0], z_r.at[fr], at_sib).wait_recv()
    total = g3r[0].astype(F32)
    for n in range(1, 8):
        total = total + g3r[n].astype(F32)
    grad_proj[...] = total[:24]

    @pl.when(active)
    def _():
        for z in range(4):
            for buf, ss in ((kb, ks_s), (vb, vs_s)):
                remote(buf.at[z * 2 + c], buf.at[z * 2 + c], ss.at[z], ks_r.at[z], at_sib).wait_send()
        for i in range(PH):
            for d in (1, 2, 3):
                remote(ob.at[i, d], at3.at[0, :PT], o_s.at[i, d], o_r.at[0, i], at_sib).wait_send()

    for cond, copy in cond_sent:

        @pl.when(cond)
        def _(copy=copy):
            copy.wait_send()

    for copy in sent:
        copy.wait_send()


def settle(a, b, c, d, a_out, b_out, c_out, d_out, a_in, b_in, c_in, d_in, sems):
    first = [
        pltpu.make_async_copy(src, dst, sems.at[n])
        for n, (src, dst) in enumerate(((a, a_in), (b, b_in), (c, c_in), (d, d_in)))
    ]
    second = [
        pltpu.make_async_copy(src, dst, sems.at[n + 4])
        for n, (src, dst) in enumerate(((a_in, a_out), (b_in, b_out), (c_in, c_out), (d_in, d_out)))
    ]
    for copy in first:
        copy.start()
    for one, two in zip(first, second):
        one.wait()
        two.start()
    for copy in second:
        copy.wait()


def on_device(patch_in, enc_weight, enc_gain, enc_bias, interp_index, queries, key_rows, value_rows, proj_weight):
    vm = pl.BlockSpec(memory_space=pltpu.VMEM)
    hbm = pl.BlockSpec(memory_space=pltpu.HBM)
    dma = pltpu.SemaphoreType.DMA
    attn, cosine, grad_attn, grad_proj = pl.pallas_call(
        kernel,
        out_shape=(
            jax.ShapeDtypeStruct((TOK, DA), BF),
            jax.ShapeDtypeStruct((1, TOK), F32),
            jax.ShapeDtypeStruct((TOK, DA), BF),
            jax.ShapeDtypeStruct((24, DA), F32),
        ),
        in_specs=[hbm] * 9,
        out_specs=(vm,) * 4,
        scratch_shapes=[
            pltpu.VMEM((192, 128), BF),
            pltpu.VMEM((192, E), BF),
            pltpu.VMEM((E,), F32),
            pltpu.VMEM((E,), F32),
            pltpu.VMEM((1, TOK), jnp.int32),
            pltpu.VMEM((E, DA), BF),
            pltpu.VMEM((NH, TOK, HD), BF),
            pltpu.VMEM((NH, TOK, HD), BF),
            pltpu.VMEM((NH, TOK, HD), BF),
            pltpu.VMEM((PH, 4, PT, HD), BF),
            pltpu.VMEM((8, TOK, HD), BF),
            pltpu.VMEM((8, TOK, HD), BF),
            pltpu.VMEM((PH, 4, PT, HD), BF),
            pltpu.VMEM((NH, TOK, HD), BF),
            pltpu.VMEM((2, 4, 16, E), F32),
            pltpu.VMEM((4, 16, E), F32),
            pltpu.VMEM((4, 16, E), BF),
            pltpu.VMEM((4, 16, E), BF),
            pltpu.VMEM((4, 4, 16, EC), BF),
            pltpu.VMEM((8, 2, 4, 16, EC), BF),
            pltpu.VMEM((TOK, EC), F32),
            pltpu.VMEM((PH, 8, SUB, EC), F32),
            pltpu.VMEM((PH, 2, 2, SUB, EC), BF),
            pltpu.VMEM((PH, 2, 2, SUB, EC), BF),
            pltpu.VMEM((PH, SUB, EC), BF),
            pltpu.VMEM((PH, SUB, EC), BF),
            pltpu.VMEM((PH, 2, SUB, EC), BF),
            pltpu.VMEM((PH, 2, SUB, EC), BF),
            pltpu.VMEM((PH, 8, SUB, EC), BF),
            pltpu.VMEM((PH, 4, 8, 128), F32),
            pltpu.VMEM((2, PH, 8, 128), F32),
            pltpu.VMEM((4, 2, BLK, DA), F32),
            pltpu.VMEM((4, BLK, DA), BF),
            pltpu.VMEM((4, BLK, DA), BF),
            pltpu.VMEM((3, BLK, DA), BF),
            pltpu.VMEM((4, BLK, DA), BF),
            pltpu.VMEM((8, 32, DA), BF),
            pltpu.VMEM((8, 32, DA), BF),
            dma((6,)),
            dma((3, NH)),
            dma((NH,)),
            dma((4,)),
            dma((4,)),
            dma((4,)),
            dma((NH,)),
            dma((4,)),
            dma((4,)),
            dma((4,)),
            dma((PH, NH)),
            dma((PH, 4)),
            dma((PH, 4)),
            dma((NH, PH)),
            dma((4,)),
            dma((4,)),
            dma((4,)),
            dma((4,)),
            dma((8,)),
            dma((8,)),
            dma((8,)),
            dma((8,)),
            dma((PH, 5)),
            dma((PH, 5)),
            dma((PH, 4)),
            dma((PH, 4)),
            dma((1,)),
            dma((1,)),
            dma((PH, 8)),
            dma((PH, 8)),
            dma((4,)),
            dma((4,)),
            dma((4, 4)),
            dma((4, 4)),
            dma((4, 2)),
            dma((8,)),
        ],
        compiler_params=pltpu.CompilerParams(
            collective_id=0, has_side_effects=True, vmem_limit_bytes=56 * 2**20
        ),
        name="whole",
    )(
        patch_in[0].T,
        enc_weight,
        enc_gain,
        enc_bias,
        interp_index,
        queries[0],
        key_rows[0],
        value_rows[0],
        proj_weight,
    )
    results = (attn, cosine, grad_attn, grad_proj)
    attn, cosine, grad_attn, grad_proj = pl.pallas_call(
        settle,
        out_shape=tuple(jax.ShapeDtypeStruct(a.shape, a.dtype) for a in results),
        in_specs=[hbm] * 4,
        out_specs=(hbm,) * 4,
        scratch_shapes=[pltpu.VMEM(a.shape, a.dtype) for a in results] + [dma((8,))],
        compiler_params=pltpu.CompilerParams(vmem_limit_bytes=60 * 2**20),
        name="settle",
    )(*results)
    return attn[None], cosine, grad_attn[None], grad_proj


def solution(mesh):
    placed = (
        P("dp", "head", "seq"),
        P("seq", None),
        P(),
        P(),
        P("dp", "seq"),
        P("dp", "seq", "head"),
        P("dp", "seq", "head"),
        P("dp", "seq", "head"),
        P(None, "head"),
    )
    return jax.shard_map(
        on_device,
        mesh=mesh,
        in_specs=placed,
        out_specs=(
            P("dp", "seq", "head"),
            P("dp", "seq"),
            P("dp", "seq", "head"),
            P(("dp", "seq"), "head"),
        ),
        check_vma=False,
    )
```
